256 devices in a mesh: ctx: 32 (over x, y, core), tp: 8 (over z).
Axes of the slice: x: 4, y: 4, z: 8, core: 2. Of those that a mesh axis runs over, the one named last changes fastest.
Arguments:
- tokens: bfloat16 [4096, 4096], P('ctx', 'tp'), may hold values from -6 to 6
- out_grad: bfloat16 [4096, 4096], P('ctx', 'tp'), may hold values from -6 to 6
- route_ids: int32 [4096, 8], P('ctx'), may hold values from 0 to 63, all different within a row; in each aligned block of 128 rows (0 to 127, 128 to 255, ...) at most 24 rows name the same one
- gate_vals: float32 [4096, 8], P('ctx'), may hold values from 0.03 to 0.5
- w_gate_up: bfloat16 [64, 4096, 1536], P('ctx', 'tp'), may hold values from -0.09375 to 0.09375
- w_down: bfloat16 [64, 768, 4096], P('ctx', None, 'tp'), may hold values from -0.21875 to 0.21875
Outputs:
- moe_out: bfloat16 [4096, 4096], P('ctx', 'tp')
- tokens_grad: bfloat16 [4096, 4096], P('ctx', 'tp')
- w_gate_up_grad: bfloat16 [64, 4096, 1536], P('ctx', 'tp')
- w_down_grad: bfloat16 [64, 768, 4096], P('ctx', None, 'tp')
The draws below stay inside these ranges and needn't reach their ends.
Inputs may be any that keep to these rules, and one draw needn't show every extreme that they name: `route_ids`: each token names 8 different experts. Among the 128 tokens of one index of ctx no expert is named more than 24 times, and in every draw some expert is named exactly 24 times by one such block.
All inputs are finite; a program needn't handle non-finite values.
Results may differ from the reference program's by a relative error of at most 0.0064.
Values may be sent and summed in bfloat16 or wider, within the bound.
A program may use at most 128 MiB of HBM per device.

```python
import math
import jax
import jax.numpy as jnp
import numpy as np
from jax import lax

D = 4096
FF = 768
TOPK = 8
TOK_DEV = 128
EXPERTS = 64
CAP = 24
EXPERT_ROWS = 768
TOKENS = 4096
N_CTX = 32


def shard_levels(stream_key, extent, shards, least, high):
    level, own = 1.0, jax.random.fold_in(stream_key, 6)
    for dim, parts in shards:
        steps = jnp.exp(jax.random.uniform(jax.random.fold_in(own, dim), (parts,), jnp.float32, least / len(shards), high / len(shards)))
        level = level * jnp.repeat(steps, extent[dim] // parts).reshape([-1 if axis == dim else 1 for axis in range(len(extent))])
    return level


def deal_out(own_key, own, number, rows, number_of, top, reach, lean):
    order = jax.random.permutation(own_key, number_of)
    crowded, common = shares(number_of, rows * top, reach, lean, True), shares(number_of, rows * top, reach, lean, False)
    places = jnp.arange(number_of)

    def named(sizes, turn):
        used = int((sizes > 0).sum())
        fixed = max(1, used // 4)
        passed = fixed + (places - fixed + turn * (used - fixed)) % max(1, number_of - fixed)
        return jnp.zeros((number_of,), jnp.int32).at[order[jnp.where(places < fixed, places, passed)]].set(jnp.asarray(sizes, jnp.int32))

    sizes = jnp.where(number % 4 == 0, named(crowded, number // 4), named(common, number - number // 4 - 1))
    mixed = jax.random.permutation(jax.random.fold_in(own, 3), number_of)
    source_of, taker = mixed[0:number_of // 2 * 2:2], mixed[1:number_of // 2 * 2:2]
    room = jnp.minimum(sizes[source_of] - 1, reach - sizes[taker]) // 2
    room = jnp.where((source_of == order[0]) | (taker == order[0]) | (sizes[taker] == 0), 0, jnp.maximum(room, 0))
    passed = jax.random.randint(jax.random.fold_in(own, 4), (number_of // 2,), 0, 1 << 20) % (room + 1)
    sizes = sizes.at[source_of].add(-passed).at[taker].add(passed)
    labels = jnp.searchsorted(jnp.cumsum(sizes), jnp.arange(rows * top), side="right").astype(jnp.int32)
    listing = labels.reshape(top, rows).T
    listing = listing[jax.random.permutation(jax.random.fold_in(own, 1), rows)]
    turn = jax.random.randint(jax.random.fold_in(own, 2), (rows, 1), 0, top)
    return jnp.take_along_axis(listing, (jnp.arange(top)[None, :] + turn) % top, axis=1)


def shares(number_of, total, most, lean, full):
    weights = [(1 << 20) // math.isqrt(standing ** lean) + 1 for standing in range(1, number_of + 1)]
    largest = most if full else min(most, max(-(-total // number_of), total * weights[0] // sum(weights)))
    least = 1 if total - largest >= number_of - 1 else 0
    holding, rest = [largest] + [least] * (number_of - 1), total - largest - least * (number_of - 1)
    while rest > 0:
        free = [i for i in range(1, number_of) if holding[i] < largest] or [i for i in range(1, number_of) if holding[i] < most]
        whole, remaining = sum([weights[i] for i in free]), rest
        for i in free:
            addition = min(most - holding[i], max(1, remaining * weights[i] // whole), rest)
            holding[i] = holding[i] + addition
            rest = rest - addition
    return np.array(holding)


def scatter_about(rng, dims, width, bound, shards=(), kind=jnp.bfloat16):
    loudness = shard_levels(rng, dims, shards, -0.22, 0.18) if shards else 1.0
    values = jax.random.normal(rng, dims, jnp.float32) * width * loudness
    return jnp.minimum(jnp.maximum(values, -bound), bound).astype(kind)


def setup_inputs(seed: int = 0) -> dict:
    keys = jax.random.split(jax.random.key(seed), 7)
    tokens = scatter_about(keys[0], (TOKENS, D), 1.0, 6.0, ((0, 32), (1, 8)))
    out_grad = scatter_about(keys[1], (TOKENS, D), 1.0, 6.0, ((0, 32), (1, 8)))
    route_ids_keys = jax.random.split(jax.random.fold_in(keys[2], 1), TOKENS // TOK_DEV)
    route_ids_turns = jax.random.permutation(jax.random.fold_in(keys[2], 3), TOKENS // TOK_DEV)
    route_ids = jax.vmap(lambda own, number: deal_out(jax.random.fold_in(keys[2], 2), own, number, TOK_DEV, EXPERTS, TOPK, CAP, 1))(route_ids_keys, route_ids_turns).reshape((TOKENS, TOPK))
    gate_vals = jnp.clip(jnp.exp(math.log(0.5) - 2.8134107 * jax.random.uniform(keys[3], (TOKENS, TOPK), jnp.float32) ** shard_levels(keys[3], (TOKENS, TOPK), ((0, 32),), -0.2, 0.2)), 0.03, 0.5)
    w_gate_up = scatter_about(keys[4], (EXPERTS, D, 2 * FF), D ** -0.5, 0.09375, ((0, 32), (1, 8)))
    w_down = scatter_about(keys[5], (EXPERTS, FF, D), FF ** -0.5, 0.21875, ((0, 32), (2, 8)))
    return dict(tokens=tokens, out_grad=out_grad, route_ids=route_ids, gate_vals=gate_vals, w_gate_up=w_gate_up, w_down=w_down)


def activate(gate_up):
    return (jax.nn.silu(gate_up[:, :FF]) * gate_up[:, FF:]).astype(jnp.bfloat16)

def activate_grad(gate_up, hidden_grad):
    gate_part = gate_up[:, :FF]
    up_part = gate_up[:, FF:]
    sigma = jax.nn.sigmoid(gate_part)
    gate_grad = hidden_grad * up_part * sigma * (1.0 + gate_part * (1.0 - sigma))
    up_grad = hidden_grad * jax.nn.silu(gate_part)
    return jnp.concatenate([gate_grad, up_grad], axis=1).astype(jnp.bfloat16)

def reference(tokens, out_grad, route_ids, gate_vals, w_gate_up, w_down):
    pairs = TOK_DEV * TOPK
    blocks = route_ids.reshape(N_CTX, pairs).astype(jnp.int32)
    onehot = (blocks[:, :, None] == jnp.arange(EXPERTS, dtype=jnp.int32)[None, None, :]).astype(jnp.int32)
    earlier = (jnp.cumsum(onehot, axis=1) - onehot).astype(jnp.int32)
    slot_index = lax.optimization_barrier(jnp.sum(earlier * onehot, axis=2)).astype(jnp.int32)
    source = jnp.arange(N_CTX, dtype=jnp.int32)[:, None]
    position = (blocks * EXPERT_ROWS + source * CAP + slot_index).astype(jnp.int32).reshape(-1)
    token_ids = jnp.repeat(jnp.arange(TOKENS, dtype=jnp.int32), TOPK).astype(jnp.int32)
    row_table = jnp.full((EXPERTS * EXPERT_ROWS,), TOKENS, jnp.int32).at[position].set(token_ids)
    weight_table = jnp.zeros((EXPERTS * EXPERT_ROWS,), jnp.float32).at[position].set(gate_vals.reshape(-1))
    row_table = row_table.reshape(EXPERTS, EXPERT_ROWS)
    weight_table = weight_table.reshape(EXPERTS, EXPERT_ROWS)
    blank_row = jnp.zeros((1, D), jnp.bfloat16)
    padded_tokens = jnp.concatenate([tokens, blank_row], axis=0)
    padded_grads = jnp.concatenate([out_grad, blank_row], axis=0)

    def per_expert(carry, inputs):
        moe_sum, input_sum = carry
        rows_ids, weights, gate_up_w, down_w = inputs
        expert_rows = padded_tokens[rows_ids]
        row_grads = (weights[:, None] * padded_grads[rows_ids].astype(jnp.float32)).astype(jnp.bfloat16)
        gate_up = jnp.dot(expert_rows, gate_up_w, preferred_element_type=jnp.float32)
        hidden = activate(gate_up)
        expert_out = jnp.dot(hidden, down_w, preferred_element_type=jnp.float32).astype(jnp.bfloat16)
        hidden_grad = jnp.dot(row_grads, down_w.T, preferred_element_type=jnp.float32)
        gate_up_grad = activate_grad(gate_up, hidden_grad)
        input_rows = jnp.dot(gate_up_grad, gate_up_w.T, preferred_element_type=jnp.float32).astype(jnp.bfloat16)
        grad_gate_up_w = jnp.dot(expert_rows.T, gate_up_grad, preferred_element_type=jnp.float32).astype(jnp.bfloat16)
        grad_down_w = jnp.dot(hidden.T, row_grads, preferred_element_type=jnp.float32).astype(jnp.bfloat16)
        moe_sum = moe_sum.at[rows_ids].add(weights[:, None] * expert_out.astype(jnp.float32))
        input_sum = input_sum.at[rows_ids].add(input_rows.astype(jnp.float32))
        return ((moe_sum, input_sum), (grad_gate_up_w, grad_down_w))
    start_sums = (jnp.zeros((TOKENS + 1, D), jnp.float32), jnp.zeros((TOKENS + 1, D), jnp.float32))
    (moe_sum, input_sum), (gate_up_grads, down_grads) = lax.scan(per_expert, start_sums, (row_table, weight_table, w_gate_up, w_down))
    moe_out = moe_sum[:TOKENS].astype(jnp.bfloat16)
    tokens_grad = input_sum[:TOKENS].astype(jnp.bfloat16)
    return (moe_out, tokens_grad, gate_up_grads, down_grads)
```

```python
import functools

import jax
import jax.numpy as jnp
from jax import lax
from jax.experimental import pallas as pl
from jax.experimental.pallas import tpu as pltpu
from jax.sharding import PartitionSpec as P

BF = jnp.bfloat16
F32 = jnp.float32
MESH = pl.DeviceIdType.MESH
SIDE = 4
CORES = 2
CHUNKS = 4
SPOTS = 8
RING = 8

OFFSETS = (
    ((0, 0), (1, 0), (3, 0), (0, 1)),
    ((2, 0), (0, 2), (1, 3), (2, 1)),
    ((2, 2), (1, 2), (3, 2), (2, 3)),
    ((0, 3), (1, 1), (3, 3), (3, 1)),
)


def dot(a, b, ca=1, cb=0):
    return lax.dot_general(a, b, (((ca,), (cb,)), ((), ())), preferred_element_type=F32)


def pick(chunk, values):
    result = values[-1]
    for index in range(len(values) - 2, -1, -1):
        result = jnp.where(chunk == index, values[index], result)
    return result


def kernel(
    tokens, out_grad, routes, gates, w_gu, w_dn,
    moe_out, tokens_grad, wgu_out, wdn_out,
    tg, pick_all, gate_all, pick_c, gate_hi, gate_lo,
    x_send, x_recv, rows, wgu, wdn, part, rs_send, rs_recv, act, fin, r_recv, wgu_st, wdn_st,
    ld_sem, xs_sem, xr_sem, rss_sem, rsr_sem, ags_sem, agr_sem, rts_sem, rtr_sem, out_sem,
):
    ctx = lax.axis_index("ctx")
    tp = lax.axis_index("tp")
    n_ctx = SIDE * SIDE * CORES
    core = lax.rem(ctx, CORES)
    my_y = lax.rem(ctx // CORES, SIDE)
    my_x = ctx // (CORES * SIDE)
    up = lax.rem(tp + 1, RING)
    down = lax.rem(tp + RING - 1, RING)
    tok, top = routes.shape
    width = tokens.shape[1]
    ff = wdn.shape[1]
    cap = x_send.shape[2] // 2
    block = 2 * cap
    exp_rows = n_ctx * cap
    half_rows = SPOTS * cap
    half = 3 * ff // 2
    strip = ff // 2
    experts = 2 * n_ctx

    barrier = pltpu.get_barrier_semaphore()

    def greet(i, carry):
        pl.semaphore_signal(
            barrier, inc=1, device_id=(lax.rem(ctx + 1 + i, n_ctx), tp), device_id_type=MESH
        )
        return carry

    lax.fori_loop(0, n_ctx - 1, greet, 0)
    pl.semaphore_signal(barrier, inc=1, device_id=(ctx, up), device_id_type=MESH)
    pl.semaphore_signal(barrier, inc=1, device_id=(ctx, down), device_id_type=MESH)

    loads = [
        pltpu.make_async_copy(tokens, tg.at[:, pl.ds(0, width)], ld_sem.at[0]),
        pltpu.make_async_copy(out_grad, tg.at[:, pl.ds(width, width)], ld_sem.at[1]),
        pltpu.make_async_copy(w_gu, wgu, ld_sem.at[2]),
        pltpu.make_async_copy(w_dn, wdn, ld_sem.at[3]),
    ]
    for load in loads:
        load.start()

    lanes = lax.broadcasted_iota(jnp.int32, (tok, 128), 1)
    named = jnp.zeros((tok, 128), F32)
    gate_of = jnp.zeros((tok, 128), F32)
    for k in range(top):
        hit = routes[:, k : k + 1] == lanes
        named = named + jnp.where(hit, 1.0, 0.0)
        gate_of = gate_of + jnp.where(hit, gates[:, k : k + 1], 0.0)
    named_t = named.T
    gate_t = gate_of.T[:experts]
    before = (
        lax.broadcasted_iota(jnp.int32, (tok, tok), 0)
        < lax.broadcasted_iota(jnp.int32, (tok, tok), 1)
    )
    earlier = dot(named_t.astype(BF), jnp.where(before, 1.0, 0.0).astype(BF))[:experts]
    slot = jnp.where(named_t[:experts] > 0.5, earlier, -1.0)
    group = 8
    for g in range(experts // group):
        part_slot = slot[g * group : (g + 1) * group][:, None, :]
        part_gate = gate_t[g * group : (g + 1) * group][:, None, :]
        wanted = lax.broadcasted_iota(jnp.int32, (group, cap, tok), 1).astype(F32)
        owned = part_slot == wanted
        span = pl.ds(g * group * cap, group * cap)
        pick_all[span, :] = jnp.where(owned, 1.0, 0.0).reshape(group * cap, tok).astype(BF)
        gate_all[span, :] = jnp.where(owned, part_gate, 0.0).reshape(group * cap, tok)
    loads[0].wait()
    loads[1].wait()

    def peer(chunk, q, sign):
        dx = pick(chunk, [OFFSETS[c][q][0] for c in range(CHUNKS)])
        dy = pick(chunk, [OFFSETS[c][q][1] for c in range(CHUNKS)])
        px = lax.rem(my_x + sign * dx + SIDE, SIDE)
        py = lax.rem(my_y + sign * dy + SIDE, SIDE)
        return (px * SIDE + py) * CORES

    def dispatch(chunk, i):
        q, b = i // 2, i % 2
        return pltpu.make_async_remote_copy(
            src_ref=x_send.at[chunk, i], dst_ref=x_recv.at[chunk, 2 * q + core],
            send_sem=xs_sem.at[chunk, i], recv_sem=xr_sem.at[chunk, 2 * q + core],
            device_id=(peer(chunk, q, -1) + b, tp), device_id_type=MESH,
        )

    def arrival(chunk, i):
        return pltpu.make_async_remote_copy(
            src_ref=x_send.at[chunk, i], dst_ref=x_recv.at[chunk, i],
            send_sem=xs_sem.at[chunk, i], recv_sem=xr_sem.at[chunk, i],
            device_id=(peer(chunk, i // 2, 1) + i % 2, tp), device_id_type=MESH,
        )

    def back(chunk, i):
        q, b = i // 2, i % 2
        return pltpu.make_async_remote_copy(
            src_ref=x_send.at[chunk, i], dst_ref=r_recv.at[chunk, 2 * q + core],
            send_sem=rts_sem.at[chunk, i], recv_sem=rtr_sem.at[chunk, 2 * q + core],
            device_id=(peer(chunk, q, 1) + b, tp), device_id_type=MESH,
        )

    def back_arrival(chunk, i):
        return pltpu.make_async_remote_copy(
            src_ref=x_send.at[chunk, i], dst_ref=r_recv.at[chunk, i],
            send_sem=rts_sem.at[chunk, i], recv_sem=rtr_sem.at[chunk, i],
            device_id=(peer(chunk, i // 2, -1) + i % 2, tp), device_id_type=MESH,
        )

    def remote_only(chunk, i, act_on):
        if i < 2:
            pl.when(jnp.logical_or(chunk != 0, core != i))(act_on)
        else:
            act_on()

    def build(chunk):
        for i in range(SPOTS):
            dest = peer(chunk, i // 2, -1) + i % 2
            span = pl.ds(pl.multiple_of(dest * block, block), block)
            here = pl.ds(i * block, block)
            pick_c[chunk, here, :] = pick_all[span, :]
            weights = gate_all[span, :]
            high = weights.astype(BF)
            gate_hi[chunk, here, :] = high
            gate_lo[chunk, here, :] = (weights - high.astype(F32)).astype(BF)
            fin[pl.ds(i * block, block), 0:1] = jnp.sum(weights, axis=1, keepdims=True)
        chosen = dot(pick_c[chunk], tg[:, 0:width])
        x_send[chunk, :, :, 0:width] = chosen.astype(BF).reshape(SPOTS, block, width)
        chosen = dot(pick_c[chunk], tg[:, width : 2 * width]) * fin[:, 0:1]
        x_send[chunk, :, :, width : 2 * width] = chosen.astype(BF).reshape(SPOTS, block, width)

    def send_rows(chunk):
        for i in range(SPOTS):
            remote_only(chunk, i, lambda i=i: dispatch(chunk, i).start())

    def take_rows(chunk):
        for i in range(SPOTS):
            remote_only(chunk, i, lambda i=i: arrival(chunk, i).wait_recv())
        for pair in range(SPOTS // 2):
            first = x_recv[chunk, 2 * pair].astype(F32)
            second = x_recv[chunk, 2 * pair + 1].astype(F32)
            for e in range(2):
                both = jnp.concatenate(
                    [first[e * cap : (e + 1) * cap], second[e * cap : (e + 1) * cap]], axis=0
                )
                start = e * exp_rows + chunk * half_rows + pair * block
                rows[pl.ds(pl.multiple_of(start, 16), block), :] = both.astype(BF)

    def products(chunk):
        side = lax.rem(chunk, 2)
        for e in range(2):
            span = pl.ds(pl.multiple_of(e * exp_rows + chunk * half_rows, 16), half_rows)
            out = pl.ds(e * half_rows, half_rows)
            left = rows[span, 0:width]
            for n in range(4):
                cols = slice(n * strip, (n + 1) * strip)
                part[side, out, cols] = dot(left, wgu[e, :, cols])
            left = rows[span, width : 2 * width]
            for n in range(2):
                part[side, out, (4 + n) * strip : (5 + n) * strip] = dot(
                    left, wdn[e, n * strip : (n + 1) * strip, :], 1, 1
                )

    def own_rows(owner):
        return pl.ds(pl.multiple_of(owner * block, block), block)

    def rs_copy(chunk, way, step):
        side = lax.rem(chunk, 2)
        src, dst = rs_send.at[side, way, step], rs_recv.at[chunk, way, step]
        if step == 0:
            src, dst = src.at[way], dst.at[way]
        return pltpu.make_async_remote_copy(
            src_ref=src, dst_ref=dst,
            send_sem=rss_sem.at[chunk, way, step], recv_sem=rsr_sem.at[chunk, way, step],
            device_id=(ctx, (up, down)[way]), device_id_type=MESH,
        )

    def rs_drain(chunk):
        for way in range(2):
            for step in range(4):
                rs_copy(chunk, way, step).wait_send()

    def rs_first(chunk):
        side = lax.rem(chunk, 2)
        pl.when(chunk >= 2)(lambda: rs_drain(chunk - 2))
        owner = lax.rem(tp + 4, RING)
        for way in range(2):
            rs_send[side, way, 0, way] = part[
                side, own_rows(owner), way * half : (way + 1) * half
            ].astype(BF)
            rs_copy(chunk, way, 0).start()

    def rs_step(chunk, step):
        side = lax.rem(chunk, 2)
        for way in range(2):
            owner = lax.rem(tp + (4 - step if way == 0 else 4 + step), RING)
            rs_copy(chunk, way, step - 1).wait_recv()
            for h in range(2):
                value = part[side, own_rows(owner), h * half : (h + 1) * half]
                if step > 1 or h == way:
                    value = value + rs_recv[chunk, way, step - 1, h].astype(F32)
                rs_send[side, way, step, h] = value.astype(BF)
            rs_copy(chunk, way, step).start()

    def act_rows(chunk, owner):
        start = (owner // 4) * exp_rows + chunk * half_rows + lax.rem(owner, 4) * block
        return pl.ds(pl.multiple_of(start, 16), block)

    def rs_last(chunk):
        side = lax.rem(chunk, 2)
        for way in range(2):
            rs_copy(chunk, way, 3).wait_recv()

        def total(s):
            h, at = s // 3, (s % 3) * strip
            value = part[side, own_rows(tp), s * strip : (s + 1) * strip]
            for way in range(2):
                value = value + rs_recv[chunk, way, 3, h, :, at : at + strip].astype(F32)
            return value

        out = act_rows(chunk, tp)
        for t in range(2):
            gate, upper, grad = total(t), total(2 + t), total(4 + t)
            sigma = jax.nn.sigmoid(gate)
            silu = gate * sigma
            act[out, t * strip : (t + 1) * strip] = (silu * upper).astype(BF)
            act[out, (2 + t) * strip : (3 + t) * strip] = (
                grad * upper * sigma * (1.0 + gate * (1.0 - sigma))
            ).astype(BF)
            act[out, (4 + t) * strip : (5 + t) * strip] = (grad * silu).astype(BF)

    def ag_copy(chunk, way, step):
        owner = lax.rem(tp + (RING - step if way == 0 else step), RING)
        span = act_rows(chunk, owner)
        ref = act.at[span, :] if step < 3 else act.at[span, pl.ds(way * half, half)]
        return pltpu.make_async_remote_copy(
            src_ref=ref, dst_ref=ref,
            send_sem=ags_sem.at[chunk, way, step], recv_sem=agr_sem.at[chunk, way, step],
            device_id=(ctx, (up, down)[way]), device_id_type=MESH,
        )

    def ag_arrival(chunk, way, step):
        owner = lax.rem(tp + (2 * RING - step - 1 if way == 0 else step + 1), RING)
        span = act_rows(chunk, owner)
        ref = act.at[span, :] if step < 3 else act.at[span, pl.ds(way * half, half)]
        return pltpu.make_async_remote_copy(
            src_ref=ref, dst_ref=ref,
            send_sem=ags_sem.at[chunk, way, step], recv_sem=agr_sem.at[chunk, way, step],
            device_id=(ctx, (up, down)[way]), device_id_type=MESH,
        )

    def ag_step(chunk, step):
        for way in range(2):
            if step > 0:
                ag_arrival(chunk, way, step - 1).wait_recv()
            ag_copy(chunk, way, step).start()

    def ag_last(chunk):
        for way in range(2):
            ag_arrival(chunk, way, 3).wait_recv()

    def finish(chunk):
        for i in range(SPOTS):
            remote_only(chunk, i, lambda i=i: dispatch(chunk, i).wait_send())
        for e in range(2):
            span = pl.ds(pl.multiple_of(e * exp_rows + chunk * half_rows, 16), half_rows)
            out = pl.ds(e * half_rows, half_rows)
            fin[out, 0:width] = dot(act[span, 0:ff], wdn[e])
            fin[out, width : 2 * width] = dot(act[span, ff : 3 * ff], wgu[e], 1, 1)
        for i in range(SPOTS):
            both = jnp.concatenate(
                [
                    fin[i * cap : (i + 1) * cap, :],
                    fin[half_rows + i * cap : half_rows + (i + 1) * cap, :],
                ],
                axis=0,
            )
            x_send[chunk, i] = both.astype(BF)
            remote_only(chunk, i, lambda i=i: back(chunk, i).start())

    build(0)
    pl.semaphore_wait(barrier, n_ctx + 1)
    send_rows(0)
    x_recv[0, core] = x_send[0, core]
    build(1)
    loads[2].wait()
    loads[3].wait()
    take_rows(0)
    products(0)
    rs_first(0)
    send_rows(1)

    def phase(i, carry):
        summing = i < CHUNKS
        gathering = i >= 1

        @pl.when(i + 2 < CHUNKS)
        def _():
            build(i + 2)
            send_rows(i + 2)

        pl.when(gathering)(lambda: ag_step(i - 1, 1))
        pl.when(summing)(lambda: rs_step(i, 1))

        @pl.when(i + 1 < CHUNKS)
        def _():
            take_rows(i + 1)
            products(i + 1)
            rs_first(i + 1)

        pl.when(gathering)(lambda: ag_step(i - 1, 2))
        pl.when(summing)(lambda: rs_step(i, 2))
        pl.when(i >= 2)(lambda: finish(i - 2))
        pl.when(gathering)(lambda: ag_step(i - 1, 3))
        pl.when(summing)(lambda: rs_step(i, 3))

        @pl.when(summing)
        def _():
            rs_last(i)
            ag_step(i, 0)

        pl.when(gathering)(lambda: ag_last(i - 1))
        return carry

    lax.fori_loop(0, CHUNKS + 1, phase, 0)
    finish(CHUNKS - 1)
    r_recv[0, core] = x_send[0, core]

    stores = []
    for e in range(2):
        span = slice(e * exp_rows, (e + 1) * exp_rows)
        for n in range(2):
            cols = slice(n * ff, (n + 1) * ff)
            wgu_st[e, :, cols] = dot(
                rows[span, 0:width], act[span, (1 + n) * ff : (2 + n) * ff], 0, 0
            ).astype(BF)
        stores.append(pltpu.make_async_copy(wgu_st.at[e], wgu_out.at[e], out_sem.at[e]))
        stores[-1].start()
        wdn_st[e] = dot(act[span, 0:ff], rows[span, width : 2 * width], 0, 0).astype(BF)
        stores.append(pltpu.make_async_copy(wdn_st.at[e], wdn_out.at[e], out_sem.at[2 + e]))
        stores[-1].start()

    out_sum = jnp.zeros((tok, width), F32)
    in_sum = jnp.zeros((tok, width), F32)
    for chunk in range(CHUNKS):
        for i in range(SPOTS):
            remote_only(chunk, i, lambda i=i, chunk=chunk: back_arrival(chunk, i).wait_recv())
        came = r_recv[chunk, :, :, 0:width].reshape(SPOTS * block, width)
        out_sum = out_sum + dot(gate_hi[chunk], came, 0, 0) + dot(gate_lo[chunk], came, 0, 0)
        came = r_recv[chunk, :, :, width : 2 * width].reshape(SPOTS * block, width)
        in_sum = in_sum + dot(pick_c[chunk], came, 0, 0)
    moe_out[...] = out_sum.astype(BF)
    tokens_grad[...] = in_sum.astype(BF)

    for chunk in range(CHUNKS):
        for way in range(2):
            for step in range(4):
                ag_copy(chunk, way, step).wait_send()
        for i in range(SPOTS):
            remote_only(chunk, i, lambda i=i, chunk=chunk: back(chunk, i).wait_send())
    rs_drain(CHUNKS - 2)
    rs_drain(CHUNKS - 1)
    for store in stores:
        store.wait()


def body(tokens, out_grad, routes, gates, w_gu, w_dn):
    tok, width = tokens.shape
    top = routes.shape[1]
    ff = w_dn.shape[1]
    n_ctx = SIDE * SIDE * CORES
    cap = 3 * tok * top // (4 * n_ctx)
    block = 2 * cap
    chunk_rows = SPOTS * block
    all_rows = CHUNKS * chunk_rows
    half = 3 * ff // 2
    dma = pltpu.SemaphoreType.DMA
    any_space = pl.BlockSpec(memory_space=pl.ANY)
    vmem = pl.BlockSpec(memory_space=pltpu.VMEM)
    flops = 6 * all_rows * width * 3 * ff
    return pl.pallas_call(
        kernel,
        out_shape=(
            jax.ShapeDtypeStruct((tok, width), BF),
            jax.ShapeDtypeStruct((tok, width), BF),
            jax.ShapeDtypeStruct(w_gu.shape, BF),
            jax.ShapeDtypeStruct(w_dn.shape, BF),
        ),
        in_specs=[any_space, any_space, vmem, vmem, any_space, any_space],
        out_specs=(vmem, vmem, any_space, any_space),
        scratch_shapes=[
            pltpu.VMEM((tok, 2 * width), BF),
            pltpu.VMEM((all_rows, tok), BF),
            pltpu.VMEM((all_rows, tok), F32),
            pltpu.VMEM((CHUNKS, chunk_rows, tok), BF),
            pltpu.VMEM((CHUNKS, chunk_rows, tok), BF),
            pltpu.VMEM((CHUNKS, chunk_rows, tok), BF),
            pltpu.VMEM((CHUNKS, SPOTS, block, 2 * width), BF),
            pltpu.VMEM((CHUNKS, SPOTS, block, 2 * width), BF),
            pltpu.VMEM((all_rows, 2 * width), BF),
            pltpu.VMEM(w_gu.shape, BF),
            pltpu.VMEM(w_dn.shape, BF),
            pltpu.VMEM((2, chunk_rows, 3 * ff), F32),
            pltpu.VMEM((2, 2, 4, 2, block, half), BF),
            pltpu.VMEM((CHUNKS, 2, 4, 2, block, half), BF),
            pltpu.VMEM((all_rows, 3 * ff), BF),
            pltpu.VMEM((chunk_rows, 2 * width), F32),
            pltpu.VMEM((CHUNKS, SPOTS, block, 2 * width), BF),
            pltpu.VMEM(w_gu.shape, BF),
            pltpu.VMEM(w_dn.shape, BF),
            dma((4,)),
            dma((CHUNKS, SPOTS)),
            dma((CHUNKS, SPOTS)),
            dma((CHUNKS, 2, 4)),
            dma((CHUNKS, 2, 4)),
            dma((CHUNKS, 2, 4)),
            dma((CHUNKS, 2, 4)),
            dma((CHUNKS, SPOTS)),
            dma((CHUNKS, SPOTS)),
            dma((4,)),
        ],
        compiler_params=pltpu.CompilerParams(
            collective_id=0, has_side_effects=True, vmem_limit_bytes=60 * 1024 * 1024
        ),
        cost_estimate=pl.CostEstimate(flops=flops, bytes_accessed=10 << 20, transcendentals=0),
        name="moe",
    )(tokens, out_grad, routes, gates, w_gu, w_dn)


def solution(mesh):
    return jax.shard_map(
        body,
        mesh=mesh,
        in_specs=(
            P("ctx", "tp"),
            P("ctx", "tp"),
            P("ctx", None),
            P("ctx", None),
            P("ctx", "tp", None),
            P("ctx", None, "tp"),
        ),
        out_specs=(P("ctx", "tp"), P("ctx", "tp"), P("ctx", "tp", None), P("ctx", None, "tp")),
        check_vma=False,
    )
```

```python
import functools

import jax
import jax.numpy as jnp
from jax import lax
from jax.experimental import pallas as pl
from jax.experimental.pallas import tpu as pltpu
from jax.sharding import PartitionSpec as P

BF = jnp.bfloat16
F32 = jnp.float32
MESH = pl.DeviceIdType.MESH
SIDE = 4
CORES = 2
CHUNKS = 4
SPOTS = 8
RING = 8

OFFSETS = (
    ((0, 0), (1, 0), (3, 0), (0, 1)),
    ((2, 0), (0, 2), (2, 2), (3, 3)),
    ((2, 1), (2, 3), (1, 2), (3, 2)),
    ((0, 3), (1, 1), (3, 1), (1, 3)),
)


def dot(a, b, ca=1, cb=0):
    return lax.dot_general(a, b, (((ca,), (cb,)), ((), ())), preferred_element_type=F32)


def pick(chunk, values):
    result = values[-1]
    for index in range(len(values) - 2, -1, -1):
        result = jnp.where(chunk == index, values[index], result)
    return result


def kernel(
    tokens, out_grad, routes, gates, w_gu, w_dn,
    moe_out, tokens_grad, wgu_out, wdn_out,
    tg, pick_all, gate_all, pick_c, gate_hi, gate_lo,
    x_send, x_recv, rows, wgu, wdn, part, rs_send, rs_recv, act, fin, r_recv, wgu_st, wdn_st,
    ld_sem, xs_sem, xr_sem, rss_sem, rsr_sem, ags_sem, agr_sem, rts_sem, rtr_sem, out_sem,
):
    ctx = lax.axis_index("ctx")
    tp = lax.axis_index("tp")
    n_ctx = SIDE * SIDE * CORES
    core = lax.rem(ctx, CORES)
    my_y = lax.rem(ctx // CORES, SIDE)
    my_x = ctx // (CORES * SIDE)
    up = lax.rem(tp + 1, RING)
    down = lax.rem(tp + RING - 1, RING)
    top, tok = routes.shape
    width = tokens.shape[1]
    ff = wdn.shape[1]
    cap = x_send.shape[2] // 2
    block = 2 * cap
    exp_rows = n_ctx * cap
    half_rows = SPOTS * cap
    strip = ff // 2
    wide = 3 * strip
    cuts = ((wide // 128 + 1) // 2 * 128, wide // 256 * 128)
    experts = 2 * n_ctx

    barrier = pltpu.get_barrier_semaphore()

    def greet(i, carry):
        pl.semaphore_signal(
            barrier, inc=1, device_id=(lax.rem(ctx + 1 + i, n_ctx), tp), device_id_type=MESH
        )
        return carry

    lax.fori_loop(0, n_ctx - 1, greet, 0)
    pl.semaphore_signal(barrier, inc=1, device_id=(ctx, up), device_id_type=MESH)
    pl.semaphore_signal(barrier, inc=1, device_id=(ctx, down), device_id_type=MESH)

    loads = [
        pltpu.make_async_copy(tokens, tg.at[:, pl.ds(0, width)], ld_sem.at[0]),
        pltpu.make_async_copy(out_grad, tg.at[:, pl.ds(width, width)], ld_sem.at[1]),
        pltpu.make_async_copy(w_dn, wdn, ld_sem.at[2]),
    ]
    for t in range(2):
        for u in range(2):
            loads.append(
                pltpu.make_async_copy(
                    w_gu.at[:, :, pl.ds(u * ff + t * strip, strip)],
                    wgu.at[:, :, pl.ds(t * ff + u * strip, strip)],
                    ld_sem.at[3 + 2 * t + u],
                )
            )
    for load in loads:
        load.start()

    ids = lax.broadcasted_iota(jnp.int32, (experts, tok), 0)
    named = jnp.zeros((experts, tok), F32)
    gate_t = jnp.zeros((experts, tok), F32)
    for k in range(top):
        hit = routes[k : k + 1, :] == ids
        named = named + jnp.where(hit, 1.0, 0.0)
        gate_t = gate_t + jnp.where(hit, gates[k : k + 1, :], 0.0)
    before = (
        lax.broadcasted_iota(jnp.int32, (tok, tok), 0)
        < lax.broadcasted_iota(jnp.int32, (tok, tok), 1)
    )
    earlier = dot(named.astype(BF), jnp.where(before, 1.0, 0.0).astype(BF))
    slot = jnp.where(named > 0.5, earlier, -1.0)
    group = 8
    for g in range(experts // group):
        part_slot = slot[g * group : (g + 1) * group][:, None, :]
        part_gate = gate_t[g * group : (g + 1) * group][:, None, :]
        wanted = lax.broadcasted_iota(jnp.int32, (group, cap, tok), 1).astype(F32)
        owned = part_slot == wanted
        span = pl.ds(g * group * cap, group * cap)
        pick_all[span, :] = jnp.where(owned, 1.0, 0.0).reshape(group * cap, tok).astype(BF)
        gate_all[span, :] = jnp.where(owned, part_gate, 0.0).reshape(group * cap, tok)
    loads[0].wait()
    loads[1].wait()

    def peer(chunk, q, sign):
        if isinstance(q, int):
            dx = pick(chunk, [OFFSETS[c][q][0] for c in range(CHUNKS)])
            dy = pick(chunk, [OFFSETS[c][q][1] for c in range(CHUNKS)])
        else:
            dx = pick(q, [offset[0] for offset in OFFSETS[chunk]])
            dy = pick(q, [offset[1] for offset in OFFSETS[chunk]])
        px = lax.rem(my_x + sign * dx + SIDE, SIDE)
        py = lax.rem(my_y + sign * dy + SIDE, SIDE)
        return (px * SIDE + py) * CORES

    def dispatch(chunk, i):
        q, b = i // 2, i % 2
        return pltpu.make_async_remote_copy(
            src_ref=x_send.at[chunk, i], dst_ref=x_recv.at[chunk, 2 * q + core],
            send_sem=xs_sem.at[chunk, i], recv_sem=xr_sem.at[chunk, 2 * q + core],
            device_id=(peer(chunk, q, -1) + b, tp), device_id_type=MESH,
        )

    def arrival(chunk, i):
        return pltpu.make_async_remote_copy(
            src_ref=x_send.at[chunk, i], dst_ref=x_recv.at[chunk, i],
            send_sem=xs_sem.at[chunk, i], recv_sem=xr_sem.at[chunk, i],
            device_id=(peer(chunk, i // 2, 1) + i % 2, tp), device_id_type=MESH,
        )

    def back(chunk, i, q=None):
        q, b = i // 2 if q is None else q, i % 2
        i = 2 * q + b
        return pltpu.make_async_remote_copy(
            src_ref=x_send.at[chunk, i], dst_ref=r_recv.at[chunk, 2 * q + core],
            send_sem=rts_sem.at[chunk, i], recv_sem=rtr_sem.at[chunk, 2 * q + core],
            device_id=(peer(chunk, q, 1) + b, tp), device_id_type=MESH,
        )

    def back_arrival(chunk, i):
        return pltpu.make_async_remote_copy(
            src_ref=x_send.at[chunk, i], dst_ref=r_recv.at[chunk, i],
            send_sem=rts_sem.at[chunk, i], recv_sem=rtr_sem.at[chunk, i],
            device_id=(peer(chunk, i // 2, -1) + i % 2, tp), device_id_type=MESH,
        )

    def remote_only(chunk, i, act_on):
        if i < 2:
            pl.when(jnp.logical_or(chunk != 0, core != i))(act_on)
        else:
            act_on()

    def build(chunk):
        for i in range(SPOTS):
            dest = peer(chunk, i // 2, -1) + i % 2
            span = pl.ds(pl.multiple_of(dest * block, block), block)
            here = pl.ds(i * block, block)
            pick_c[chunk, here, :] = pick_all[span, :]
            weights = gate_all[span, :]
            high = weights.astype(BF)
            gate_hi[chunk, here, :] = high
            gate_lo[chunk, here, :] = (weights - high.astype(F32)).astype(BF)
            fin[pl.ds(i * block, block), 0:1] = jnp.sum(weights, axis=1, keepdims=True)
        chosen = dot(pick_c[chunk], tg[:, 0:width])
        x_send[chunk, :, :, 0:width] = chosen.astype(BF).reshape(SPOTS, block, width)
        chosen = dot(pick_c[chunk], tg[:, width : 2 * width]) * fin[:, 0:1]
        x_send[chunk, :, :, width : 2 * width] = chosen.astype(BF).reshape(SPOTS, block, width)

    def send_rows(chunk):
        for i in range(SPOTS):
            remote_only(chunk, i, lambda i=i: dispatch(chunk, i).start())

    def take_rows(chunk):
        for i in range(SPOTS):
            remote_only(chunk, i, lambda i=i: arrival(chunk, i).wait_recv())
        for pair in range(SPOTS // 2):
            first = x_recv[chunk, 2 * pair].astype(F32)
            second = x_recv[chunk, 2 * pair + 1].astype(F32)
            for e in range(2):
                both = jnp.concatenate(
                    [first[e * cap : (e + 1) * cap], second[e * cap : (e + 1) * cap]], axis=0
                )
                start = e * exp_rows + chunk * half_rows + pair * block
                rows[pl.ds(pl.multiple_of(start, 16), block), :] = both.astype(BF)

    def products(chunk):
        side = lax.rem(chunk, 2)
        for e in range(2):
            span = pl.ds(pl.multiple_of(e * exp_rows + chunk * half_rows, 16), half_rows)
            out = pl.ds(e * half_rows, half_rows)
            left, grads = rows[span, 0:width], rows[span, width : 2 * width]
            for t in range(2):
                part[side, t, out, 0 : 2 * strip] = dot(left, wgu[e, :, t * ff : (t + 1) * ff])
                part[side, t, out, 2 * strip : wide] = dot(
                    grads, wdn[e, t * strip : (t + 1) * strip, :], 1, 1
                )

    def own_rows(owner):
        return pl.ds(pl.multiple_of(owner * block, block), block)

    def cut(t, way):
        return pl.ds(0, cuts[t]) if way == 0 else pl.ds(cuts[t], wide - cuts[t])

    def rs_copy(chunk, t, way, step):
        side = lax.rem(chunk, 2)
        src, dst = rs_send.at[side, t, way, step], rs_recv.at[chunk, t, way, step]
        if step == 0:
            src, dst = src.at[:, cut(t, way)], dst.at[:, cut(t, way)]
        return pltpu.make_async_remote_copy(
            src_ref=src, dst_ref=dst,
            send_sem=rss_sem.at[chunk, t, way, step], recv_sem=rsr_sem.at[chunk, t, way, step],
            device_id=(ctx, (up, down)[way]), device_id_type=MESH,
        )

    def rs_drain(chunk, t):
        for way in range(2):
            for step in range(4):
                rs_copy(chunk, t, way, step).wait_send()

    def rs_step(chunk, t, step):
        side = lax.rem(chunk, 2)
        if step == 0:
            pl.when(chunk >= 2)(lambda: rs_drain(chunk - 2, t))
        for way in range(2):
            owner = lax.rem(tp + (4 - step if way == 0 else 4 + step), RING)
            mine = own_rows(owner)
            if step == 0:
                cols = cut(t, way)
                rs_send[side, t, way, 0, :, cols] = part[side, t, mine, cols].astype(BF)
            else:
                rs_copy(chunk, t, way, step - 1).wait_recv()
                for w in range(2):
                    cols = cut(t, w)
                    value = part[side, t, mine, cols]
                    if step > 1 or w == way:
                        value = value + rs_recv[chunk, t, way, step - 1, :, cols].astype(F32)
                    rs_send[side, t, way, step, :, cols] = value.astype(BF)
            rs_copy(chunk, t, way, step).start()

    def act_rows(chunk, owner):
        start = (owner // 4) * exp_rows + chunk * half_rows + lax.rem(owner, 4) * block
        return pl.ds(pl.multiple_of(start, 16), block)

    def rs_last(chunk, t):
        side = lax.rem(chunk, 2)
        for way in range(2):
            rs_copy(chunk, t, way, 3).wait_recv()

        def total(s):
            cols = slice(s * strip, (s + 1) * strip)
            value = part[side, t, own_rows(tp), cols]
            for way in range(2):
                value = value + rs_recv[chunk, t, way, 3, :, cols].astype(F32)
            return value

        out = act_rows(chunk, tp)
        gate, upper, grad = total(0), total(1), total(2)
        sigma = jax.nn.sigmoid(gate)
        silu = gate * sigma
        act[t, out, 0:strip] = (silu * upper).astype(BF)
        act[t, out, strip : 2 * strip] = (
            grad * upper * sigma * (1.0 + gate * (1.0 - sigma))
        ).astype(BF)
        act[t, out, 2 * strip : wide] = (grad * silu).astype(BF)

    def ag_move(chunk, t, way, step, owner):
        ref = act.at[t, act_rows(chunk, lax.rem(owner, RING))]
        if step == 3:
            ref = ref.at[:, cut(t, way)]
        return pltpu.make_async_remote_copy(
            src_ref=ref, dst_ref=ref,
            send_sem=ags_sem.at[chunk, t, way, step], recv_sem=agr_sem.at[chunk, t, way, step],
            device_id=(ctx, (up, down)[way]), device_id_type=MESH,
        )

    def ag_copy(chunk, t, way, step):
        return ag_move(chunk, t, way, step, tp + (RING - step if way == 0 else step))

    def ag_arrival(chunk, t, way, step):
        return ag_move(chunk, t, way, step, tp + (RING - step - 1 if way == 0 else step + 1))

    def ag_step(chunk, t, step):
        if step == 0:
            rs_last(chunk, t)
        for way in range(2):
            if step > 0:
                ag_arrival(chunk, t, way, step - 1).wait_recv()
            ag_copy(chunk, t, way, step).start()

    def ag_last(chunk, t):
        for way in range(2):
            ag_arrival(chunk, t, way, 3).wait_recv()

    def rows_out(e, span):
        outs = dot(act[0, span, 0:strip], wdn[e, 0:strip, :]) + dot(
            act[1, span, 0:strip], wdn[e, strip : 2 * strip, :]
        )
        grads = dot(act[0, span, strip:wide], wgu[e, :, 0:ff], 1, 1) + dot(
            act[1, span, strip:wide], wgu[e, :, ff : 2 * ff], 1, 1
        )
        return outs, grads

    def finish_pair(q):
        chunk = CHUNKS - 1
        for e in range(2):
            start = e * exp_rows + chunk * half_rows + q * block
            out = pl.ds(e * block, block)
            outs, grads = rows_out(e, pl.ds(pl.multiple_of(start, 16), block))
            fin[out, 0:width] = outs
            fin[out, width : 2 * width] = grads
        for b in range(2):
            at = b * cap
            both = jnp.concatenate([fin[at : at + cap, :], fin[block + at : block + at + cap, :]], axis=0)
            x_send[chunk, 2 * q + b] = both.astype(BF)
            back(chunk, b, q).start()

    def finish(chunk):
        ag_last(chunk, 0)
        ag_last(chunk, 1)
        for i in range(SPOTS):
            remote_only(chunk, i, lambda i=i: dispatch(chunk, i).wait_send())
        for e in range(2):
            span = pl.ds(pl.multiple_of(e * exp_rows + chunk * half_rows, 16), half_rows)
            out = pl.ds(e * half_rows, half_rows)
            outs, grads = rows_out(e, span)
            fin[out, 0:width] = outs
            fin[out, width : 2 * width] = grads
        for i in range(SPOTS):
            both = jnp.concatenate(
                [
                    fin[i * cap : (i + 1) * cap, :],
                    fin[half_rows + i * cap : half_rows + (i + 1) * cap, :],
                ],
                axis=0,
            )
            x_send[chunk, i] = both.astype(BF)
            remote_only(chunk, i, lambda i=i: back(chunk, i).start())

    build(0)
    pl.semaphore_wait(barrier, n_ctx + 1)
    send_rows(0)
    x_recv[0, core] = x_send[0, core]
    build(1)
    for load in loads[2:]:
        load.wait()
    take_rows(0)
    send_rows(1)
    products(0)

    def turn(c, carry):
        for t in range(2):
            before_c = c - 1 if t == 0 else c
            for a in range(2):

                @pl.when(jnp.logical_and(before_c >= 1, before_c <= CHUNKS))
                def _():
                    ag_step(before_c - 1, 1 - t, 2 + a)

                @pl.when(jnp.logical_and(c >= 1, c <= CHUNKS))
                def _():
                    ag_step(c - 1, t, a)

                @pl.when(jnp.logical_and(before_c >= 0, before_c < CHUNKS))
                def _():
                    rs_step(before_c, 1 - t, 2 + a)

                @pl.when(c < CHUNKS)
                def _():
                    rs_step(c, t, a)

                if (t, a) == (1, 0):

                    @pl.when(c + 2 < CHUNKS)
                    def _():
                        build(c + 2)
                        send_rows(c + 2)

                    pl.when(c >= 2)(lambda: finish(c - 2))

                if (t, a) == (1, 1):

                    @pl.when(c + 1 < CHUNKS)
                    def _():
                        take_rows(c + 1)
                        products(c + 1)

        return carry

    lax.fori_loop(0, CHUNKS + 1, turn, 0)

    stores = []

    def store(src, dst):
        stores.append(pltpu.make_async_copy(src, dst, out_sem.at[len(stores)]))
        stores[-1].start()

    def weight_grads(t):
        for e in range(2):
            span = slice(e * exp_rows, (e + 1) * exp_rows)
            wgu_st[e, :, t * ff : (t + 1) * ff] = dot(
                rows[span, 0:width], act[t, span, strip:wide], 0, 0
            ).astype(BF)
            for u in range(2):
                store(
                    wgu_st.at[e, :, pl.ds(t * ff + u * strip, strip)],
                    wgu_out.at[e, :, pl.ds(u * ff + t * strip, strip)],
                )
            wdn_st[e, t * strip : (t + 1) * strip, :] = dot(
                act[t, span, 0:strip], rows[span, width : 2 * width], 0, 0
            ).astype(BF)
            at = pl.ds(t * strip, strip)
            store(wdn_st.at[e, at], wdn_out.at[e, at])

    def combine(chunk):
        for i in range(SPOTS):
            remote_only(chunk, i, lambda: back_arrival(chunk, i).wait_recv())
        came = r_recv[chunk, :, :, 0:width].reshape(SPOTS * block, width)
        outs = dot(gate_hi[chunk], came, 0, 0) + dot(gate_lo[chunk], came, 0, 0)
        came = r_recv[chunk, :, :, width : 2 * width].reshape(SPOTS * block, width)
        grads = dot(pick_c[chunk], came, 0, 0)
        if chunk > 0:
            outs, grads = fin[0:tok, 0:width] + outs, fin[0:tok, width : 2 * width] + grads
        return outs, grads

    last = CHUNKS - 1
    for i in range(SPOTS):
        dispatch(last, i).wait_send()
    ag_step(last, 1, 2)
    ag_last(last, 0)
    finish_pair(lax.rem(tp + 2, 4))
    ag_step(last, 1, 3)
    finish_pair(lax.rem(tp + 1, 4))
    finish_pair(lax.rem(tp + 3, 4))
    weight_grads(0)
    ag_last(last, 1)
    finish_pair(lax.rem(tp, 4))
    weight_grads(1)

    r_recv[0, core] = x_send[0, core]
    for chunk in range(CHUNKS):
        outs, grads = combine(chunk)
        if chunk < last:
            fin[0:tok, 0:width] = outs
            fin[0:tok, width : 2 * width] = grads
    moe_out[...] = outs.astype(BF)
    tokens_grad[...] = grads.astype(BF)

    for chunk in range(CHUNKS):
        for t in range(2):
            for way in range(2):
                for step in range(4):
                    ag_copy(chunk, t, way, step).wait_send()
        for i in range(SPOTS):
            remote_only(chunk, i, lambda i=i, chunk=chunk: back(chunk, i).wait_send())
    for chunk in range(CHUNKS - 2, CHUNKS):
        for t in range(2):
            rs_drain(chunk, t)
    for copy in stores:
        copy.wait()


def hand_on(*refs):
    count = (len(refs) - 2) // 3
    came, left = refs[-2:]
    loads, stores = [], []
    for src, dst, mid in zip(refs[:count], refs[count : 2 * count], refs[2 * count : 3 * count]):
        pieces = 8 if len(src.shape) == 3 else 1
        for piece in range(pieces):
            views = [src, mid, dst]
            if pieces > 1:
                depth = src.shape[1] // 4
                at = pl.ds(piece % 4 * depth, depth)
                views = [view.at[piece // 4, at] for view in views]
            loads.append(pltpu.make_async_copy(views[0], views[1], came.at[len(loads)]))
            stores.append(pltpu.make_async_copy(views[1], views[2], left.at[len(stores)]))
            loads[-1].start()
    for load, copy in zip(loads, stores):
        load.wait()
        copy.start()
    for copy in stores:
        copy.wait()


def body(tokens, out_grad, routes, gates, w_gu, w_dn):
    tok, width = tokens.shape
    top = routes.shape[1]
    routes, gates = routes.T, gates.T
    ff = w_dn.shape[1]
    n_ctx = SIDE * SIDE * CORES
    cap = 3 * tok * top // (4 * n_ctx)
    block = 2 * cap
    chunk_rows = SPOTS * block
    all_rows = CHUNKS * chunk_rows
    wide = 3 * ff // 2
    dma = pltpu.SemaphoreType.DMA
    any_space = pl.BlockSpec(memory_space=pl.ANY)
    vmem = pl.BlockSpec(memory_space=pltpu.VMEM)
    flops = 6 * all_rows * width * 3 * ff
    results = pl.pallas_call(
        kernel,
        out_shape=(
            jax.ShapeDtypeStruct((tok, width), BF),
            jax.ShapeDtypeStruct((tok, width), BF),
            jax.ShapeDtypeStruct(w_gu.shape, BF),
            jax.ShapeDtypeStruct(w_dn.shape, BF),
        ),
        in_specs=[any_space, any_space, vmem, vmem, any_space, any_space],
        out_specs=(vmem, vmem, any_space, any_space),
        scratch_shapes=[
            pltpu.VMEM((tok, 2 * width), BF),
            pltpu.VMEM((all_rows, tok), BF),
            pltpu.VMEM((all_rows, tok), F32),
            pltpu.VMEM((CHUNKS, chunk_rows, tok), BF),
            pltpu.VMEM((CHUNKS, chunk_rows, tok), BF),
            pltpu.VMEM((CHUNKS, chunk_rows, tok), BF),
            pltpu.VMEM((CHUNKS, SPOTS, block, 2 * width), BF),
            pltpu.VMEM((CHUNKS, SPOTS, block, 2 * width), BF),
            pltpu.VMEM((all_rows, 2 * width), BF),
            pltpu.VMEM(w_gu.shape, BF),
            pltpu.VMEM(w_dn.shape, BF),
            pltpu.VMEM((2, 2, chunk_rows, wide), F32),
            pltpu.VMEM((2, 2, 2, 4, block, wide), BF),
            pltpu.VMEM((CHUNKS, 2, 2, 4, block, wide), BF),
            pltpu.VMEM((2, all_rows, wide), BF),
            pltpu.VMEM((chunk_rows, 2 * width), F32),
            pltpu.VMEM((CHUNKS, SPOTS, block, 2 * width), BF),
            pltpu.VMEM(w_gu.shape, BF),
            pltpu.VMEM(w_dn.shape, BF),
            dma((7,)),
            dma((CHUNKS, SPOTS)),
            dma((CHUNKS, SPOTS)),
            dma((CHUNKS, 2, 2, 4)),
            dma((CHUNKS, 2, 2, 4)),
            dma((CHUNKS, 2, 2, 4)),
            dma((CHUNKS, 2, 2, 4)),
            dma((CHUNKS, SPOTS)),
            dma((CHUNKS, SPOTS)),
            dma((12,)),
        ],
        compiler_params=pltpu.CompilerParams(
            collective_id=0, has_side_effects=True, vmem_limit_bytes=60 * 1024 * 1024
        ),
        cost_estimate=pl.CostEstimate(flops=flops, bytes_accessed=10 << 20, transcendentals=0),
        name="moe",
    )(tokens, out_grad, routes, gates, w_gu, w_dn)
    return pl.pallas_call(
        hand_on,
        out_shape=tuple(jax.ShapeDtypeStruct(r.shape, r.dtype) for r in results),
        in_specs=[any_space] * 4,
        out_specs=(any_space,) * 4,
        scratch_shapes=[pltpu.VMEM(r.shape, r.dtype) for r in results] + [dma((18,)), dma((18,))],
        compiler_params=pltpu.CompilerParams(vmem_limit_bytes=60 * 1024 * 1024),
        name="hand_on",
    )(*results)


def solution(mesh):
    return jax.shard_map(
        body,
        mesh=mesh,
        in_specs=(
            P("ctx", "tp"),
            P("ctx", "tp"),
            P("ctx", None),
            P("ctx", None),
            P("ctx", "tp", None),
            P("ctx", None, "tp"),
        ),
        out_specs=(P("ctx", "tp"), P("ctx", "tp"), P("ctx", "tp", None), P("ctx", None, "tp")),
        check_vma=False,
    )
```

```python
import functools

import jax
import jax.numpy as jnp
from jax import lax
from jax.experimental import pallas as pl
from jax.experimental.pallas import tpu as pltpu
from jax.sharding import PartitionSpec as P

BF = jnp.bfloat16
F32 = jnp.float32
MESH = pl.DeviceIdType.MESH
SIDE = 4
CORES = 2
CHUNKS = 4
SPOTS = 8
RING = 8

OFFSETS = (
    ((0, 0), (1, 0), (3, 0), (0, 1)),
    ((2, 0), (0, 2), (2, 2), (3, 3)),
    ((2, 1), (2, 3), (1, 2), (3, 2)),
    ((0, 3), (1, 1), (3, 1), (1, 3)),
)


def dot(a, b, ca=1, cb=0):
    return lax.dot_general(a, b, (((ca,), (cb,)), ((), ())), preferred_element_type=F32)


def pick(chunk, values):
    result = values[-1]
    for index in range(len(values) - 2, -1, -1):
        result = jnp.where(chunk == index, values[index], result)
    return result


def kernel(
    tokens, out_grad, routes_in, gates_in, w_gu, w_dn,
    moe_out, tokens_grad, wgu_out, wdn_out,
    routes, gates, tg, pick_all, gate_all, pick_c, gate_hi, gate_lo,
    x_send, x_recv, rows, wgu, wdn, part, rs_send, rs_recv, act, fin, r_recv, wgu_st, wdn_st,
    ld_sem, xs_sem, xr_sem, rss_sem, rsr_sem, ags_sem, agr_sem, rts_sem, rtr_sem, out_sem,
):
    ctx = lax.axis_index("ctx")
    tp = lax.axis_index("tp")
    n_ctx = SIDE * SIDE * CORES
    core = lax.rem(ctx, CORES)
    my_y = lax.rem(ctx // CORES, SIDE)
    my_x = ctx // (CORES * SIDE)
    up = lax.rem(tp + 1, RING)
    down = lax.rem(tp + RING - 1, RING)
    top, tok = routes_in.shape
    width = tokens.shape[1]
    ff = wdn.shape[1]
    cap = x_send.shape[2] // 2
    block = 2 * cap
    exp_rows = n_ctx * cap
    half_rows = SPOTS * cap
    strip = ff // 2
    wide = 3 * strip
    cuts = (2 * block // 3, block // 3)
    experts = 2 * n_ctx

    barrier = pltpu.get_barrier_semaphore()

    def greet(i, carry):
        pl.semaphore_signal(
            barrier, inc=1, device_id=(lax.rem(ctx + 1 + i, n_ctx), tp), device_id_type=MESH
        )
        return carry

    lax.fori_loop(0, n_ctx - 1, greet, 0)
    pl.semaphore_signal(barrier, inc=1, device_id=(ctx, up), device_id_type=MESH)
    pl.semaphore_signal(barrier, inc=1, device_id=(ctx, down), device_id_type=MESH)

    loads = [
        pltpu.make_async_copy(tokens, tg.at[:, pl.ds(0, width)], ld_sem.at[0]),
        pltpu.make_async_copy(out_grad, tg.at[:, pl.ds(width, width)], ld_sem.at[1]),
        pltpu.make_async_copy(w_dn, wdn, ld_sem.at[2]),
    ]
    for t in range(2):
        for u in range(2):
            loads.append(
                pltpu.make_async_copy(
                    w_gu.at[:, :, pl.ds(u * ff + t * strip, strip)],
                    wgu.at[:, :, pl.ds(t * ff + u * strip, strip)],
                    ld_sem.at[3 + 2 * t + u],
                )
            )
    tables = [
        pltpu.make_async_copy(routes_in, routes, ld_sem.at[7]),
        pltpu.make_async_copy(gates_in, gates, ld_sem.at[8]),
    ]
    for load in tables + loads:
        load.start()
    for load in tables:
        load.wait()

    ids = lax.broadcasted_iota(jnp.int32, (experts, tok), 0)
    named = jnp.zeros((experts, tok), F32)
    gate_t = jnp.zeros((experts, tok), F32)
    for k in range(top):
        hit = routes[k : k + 1, :] == ids
        named = named + jnp.where(hit, 1.0, 0.0)
        gate_t = gate_t + jnp.where(hit, gates[k : k + 1, :], 0.0)
    before = (
        lax.broadcasted_iota(jnp.int32, (tok, tok), 0)
        < lax.broadcasted_iota(jnp.int32, (tok, tok), 1)
    )
    earlier = dot(named.astype(BF), jnp.where(before, 1.0, 0.0).astype(BF))
    slot = jnp.where(named > 0.5, earlier, -1.0)
    group = 8
    for g in range(experts // group):
        part_slot = slot[g * group : (g + 1) * group][:, None, :]
        part_gate = gate_t[g * group : (g + 1) * group][:, None, :]
        wanted = lax.broadcasted_iota(jnp.int32, (group, cap, tok), 1).astype(F32)
        owned = part_slot == wanted
        span = pl.ds(g * group * cap, group * cap)
        pick_all[span, :] = jnp.where(owned, 1.0, 0.0).reshape(group * cap, tok).astype(BF)
        gate_all[span, :] = jnp.where(owned, part_gate, 0.0).reshape(group * cap, tok)
    loads[0].wait()
    loads[1].wait()

    def peer(chunk, q, sign):
        if isinstance(q, int):
            dx = pick(chunk, [OFFSETS[c][q][0] for c in range(CHUNKS)])
            dy = pick(chunk, [OFFSETS[c][q][1] for c in range(CHUNKS)])
        else:
            dx = pick(q, [offset[0] for offset in OFFSETS[chunk]])
            dy = pick(q, [offset[1] for offset in OFFSETS[chunk]])
        px = lax.rem(my_x + sign * dx + SIDE, SIDE)
        py = lax.rem(my_y + sign * dy + SIDE, SIDE)
        return (px * SIDE + py) * CORES

    def dispatch(chunk, i):
        q, b = i // 2, i % 2
        return pltpu.make_async_remote_copy(
            src_ref=x_send.at[chunk, i], dst_ref=x_recv.at[chunk, 2 * q + core],
            send_sem=xs_sem.at[chunk, i], recv_sem=xr_sem.at[chunk, 2 * q + core],
            device_id=(peer(chunk, q, -1) + b, tp), device_id_type=MESH,
        )

    def arrival(chunk, i):
        return pltpu.make_async_remote_copy(
            src_ref=x_send.at[chunk, i], dst_ref=x_recv.at[chunk, i],
            send_sem=xs_sem.at[chunk, i], recv_sem=xr_sem.at[chunk, i],
            device_id=(peer(chunk, i // 2, 1) + i % 2, tp), device_id_type=MESH,
        )

    def back(chunk, i, q=None):
        q, b = i // 2 if q is None else q, i % 2
        i = 2 * q + b
        return pltpu.make_async_remote_copy(
            src_ref=x_send.at[chunk, i], dst_ref=r_recv.at[chunk, 2 * q + core],
            send_sem=rts_sem.at[chunk, i], recv_sem=rtr_sem.at[chunk, 2 * q + core],
            device_id=(peer(chunk, q, 1) + b, tp), device_id_type=MESH,
        )

    def back_arrival(chunk, i):
        return pltpu.make_async_remote_copy(
            src_ref=x_send.at[chunk, i], dst_ref=r_recv.at[chunk, i],
            send_sem=rts_sem.at[chunk, i], recv_sem=rtr_sem.at[chunk, i],
            device_id=(peer(chunk, i // 2, -1) + i % 2, tp), device_id_type=MESH,
        )

    def remote_only(chunk, i, act_on):
        if i < 2:
            pl.when(jnp.logical_or(chunk != 0, core != i))(act_on)
        else:
            act_on()

    def build(chunk):
        for i in range(SPOTS):
            dest = peer(chunk, i // 2, -1) + i % 2
            span = pl.ds(pl.multiple_of(dest * block, block), block)
            here = pl.ds(i * block, block)
            pick_c[chunk, here, :] = pick_all[span, :]
            weights = gate_all[span, :]
            high = weights.astype(BF)
            gate_hi[chunk, here, :] = high
            gate_lo[chunk, here, :] = (weights - high.astype(F32)).astype(BF)
            fin[pl.ds(i * block, block), 0:1] = jnp.sum(weights, axis=1, keepdims=True)
        chosen = dot(pick_c[chunk], tg[:, 0:width])
        x_send[chunk, :, :, 0:width] = chosen.astype(BF).reshape(SPOTS, block, width)
        chosen = dot(pick_c[chunk], tg[:, width : 2 * width]) * fin[:, 0:1]
        x_send[chunk, :, :, width : 2 * width] = chosen.astype(BF).reshape(SPOTS, block, width)

    def send_rows(chunk):
        for i in range(SPOTS):
            remote_only(chunk, i, lambda i=i: dispatch(chunk, i).start())

    def take_rows(chunk):
        for i in range(SPOTS):
            remote_only(chunk, i, lambda i=i: arrival(chunk, i).wait_recv())
        for pair in range(SPOTS // 2):
            first = x_recv[chunk, 2 * pair].astype(F32)
            second = x_recv[chunk, 2 * pair + 1].astype(F32)
            for e in range(2):
                both = jnp.concatenate(
                    [first[e * cap : (e + 1) * cap], second[e * cap : (e + 1) * cap]], axis=0
                )
                start = e * exp_rows + chunk * half_rows + pair * block
                rows[pl.ds(pl.multiple_of(start, 16), block), :] = both.astype(BF)

    def products(chunk, t):
        side = lax.rem(chunk, 2)
        for e in range(2):
            span = pl.ds(pl.multiple_of(e * exp_rows + chunk * half_rows, 16), half_rows)
            out = pl.ds(e * half_rows, half_rows)
            left, grads = rows[span, 0:width], rows[span, width : 2 * width]
            part[side, t, out, 0 : 2 * strip] = dot(left, wgu[e, :, t * ff : (t + 1) * ff])
            part[side, t, out, 2 * strip : wide] = dot(
                grads, wdn[e, t * strip : (t + 1) * strip, :], 1, 1
            )

    def own_rows(owner):
        return pl.ds(pl.multiple_of(owner * block, block), block)

    def cut(t, way):
        return (0, cuts[t]) if way == 0 else (cuts[t], block - cuts[t])

    def some(start, t, way):
        first, count = cut(t, way)
        return pl.ds(pl.multiple_of(start + first, 16), count)

    def rs_copy(chunk, t, way, step):
        side = lax.rem(chunk, 2)
        src, dst = rs_send.at[side, t, way, step], rs_recv.at[chunk, t, way, step]
        if step == 0:
            src, dst = src.at[pl.ds(*cut(t, way))], dst.at[pl.ds(*cut(t, way))]
        return pltpu.make_async_remote_copy(
            src_ref=src, dst_ref=dst,
            send_sem=rss_sem.at[chunk, t, way, step], recv_sem=rsr_sem.at[chunk, t, way, step],
            device_id=(ctx, (up, down)[way]), device_id_type=MESH,
        )

    def rs_drain(chunk, t):
        for way in range(2):
            for step in range(4):
                rs_copy(chunk, t, way, step).wait_send()

    def rs_step(chunk, t, step):
        side = lax.rem(chunk, 2)
        if step == 0:
            pl.when(chunk >= 2)(lambda: rs_drain(chunk - 2, t))
        for way in range(2):
            owner = lax.rem(tp + (4 - step if way == 0 else 4 + step), RING)
            if step > 0:
                rs_copy(chunk, t, way, step - 1).wait_recv()
            for w in range(2):
                if step == 0 and w != way:
                    continue
                value = part[side, t, some(owner * block, t, w), :]
                here = pl.ds(*cut(t, w))
                if step > 1 or (step == 1 and w == way):
                    value = value + rs_recv[chunk, t, way, step - 1, here, :].astype(F32)
                rs_send[side, t, way, step, here, :] = value.astype(BF)
            rs_copy(chunk, t, way, step).start()

    def act_start(chunk, owner):
        return (owner // 4) * exp_rows + chunk * half_rows + lax.rem(owner, 4) * block

    def act_rows(chunk, owner):
        return pl.ds(pl.multiple_of(act_start(chunk, owner), 16), block)

    def rs_last(chunk, t):
        side = lax.rem(chunk, 2)
        for way in range(2):
            rs_copy(chunk, t, way, 3).wait_recv()

        def total(s):
            cols = slice(s * strip, (s + 1) * strip)
            value = part[side, t, own_rows(tp), cols]
            for way in range(2):
                value = value + rs_recv[chunk, t, way, 3, :, cols].astype(F32)
            return value

        out = act_rows(chunk, tp)
        gate, upper, grad = total(0), total(1), total(2)
        sigma = jax.nn.sigmoid(gate)
        silu = gate * sigma
        act[t, out, 0:strip] = (silu * upper).astype(BF)
        act[t, out, strip : 2 * strip] = (
            grad * upper * sigma * (1.0 + gate * (1.0 - sigma))
        ).astype(BF)
        act[t, out, 2 * strip : wide] = (grad * silu).astype(BF)

    def ag_move(chunk, t, way, step, owner):
        start = act_start(chunk, lax.rem(owner, RING))
        ref = act.at[t, pl.ds(pl.multiple_of(start, 16), block) if step < 3 else some(start, t, way)]
        return pltpu.make_async_remote_copy(
            src_ref=ref, dst_ref=ref,
            send_sem=ags_sem.at[chunk, t, way, step], recv_sem=agr_sem.at[chunk, t, way, step],
            device_id=(ctx, (up, down)[way]), device_id_type=MESH,
        )

    def ag_copy(chunk, t, way, step):
        return ag_move(chunk, t, way, step, tp + (RING - step if way == 0 else step))

    def ag_arrival(chunk, t, way, step):
        return ag_move(chunk, t, way, step, tp + (RING - step - 1 if way == 0 else step + 1))

    def ag_step(chunk, t, step):
        if step == 0:
            rs_last(chunk, t)
        for way in range(2):
            if step > 0:
                ag_arrival(chunk, t, way, step - 1).wait_recv()
            ag_copy(chunk, t, way, step).start()

    def ag_last(chunk, t):
        for way in range(2):
            ag_arrival(chunk, t, way, 3).wait_recv()

    def rows_out(e, span):
        outs = dot(act[0, span, 0:strip], wdn[e, 0:strip, :]) + dot(
            act[1, span, 0:strip], wdn[e, strip : 2 * strip, :]
        )
        grads = dot(act[0, span, strip:wide], wgu[e, :, 0:ff], 1, 1) + dot(
            act[1, span, strip:wide], wgu[e, :, ff : 2 * ff], 1, 1
        )
        return outs, grads

    def finish_pair(q):
        chunk = CHUNKS - 1
        for e in range(2):
            start = e * exp_rows + chunk * half_rows + q * block
            out = pl.ds(e * block, block)
            outs, grads = rows_out(e, pl.ds(pl.multiple_of(start, 16), block))
            fin[out, 0:width] = outs
            fin[out, width : 2 * width] = grads
        for b in range(2):
            at = b * cap
            both = jnp.concatenate([fin[at : at + cap, :], fin[block + at : block + at + cap, :]], axis=0)
            x_send[chunk, 2 * q + b] = both.astype(BF)
            back(chunk, b, q).start()

    def finish(chunk):
        ag_last(chunk, 0)
        ag_last(chunk, 1)
        for i in range(SPOTS):
            remote_only(chunk, i, lambda i=i: dispatch(chunk, i).wait_send())
        for e in range(2):
            span = pl.ds(pl.multiple_of(e * exp_rows + chunk * half_rows, 16), half_rows)
            out = pl.ds(e * half_rows, half_rows)
            outs, grads = rows_out(e, span)
            fin[out, 0:width] = outs
            fin[out, width : 2 * width] = grads
        for i in range(SPOTS):
            both = jnp.concatenate(
                [
                    fin[i * cap : (i + 1) * cap, :],
                    fin[half_rows + i * cap : half_rows + (i + 1) * cap, :],
                ],
                axis=0,
            )
            x_send[chunk, i] = both.astype(BF)
            remote_only(chunk, i, lambda i=i: back(chunk, i).start())

    build(0)
    pl.semaphore_wait(barrier, n_ctx + 1)
    send_rows(0)
    x_recv[0, core] = x_send[0, core]
    build(1)
    for load in loads[2:]:
        load.wait()
    take_rows(0)
    send_rows(1)
    products(0, 0)

    def turn(c, carry):
        for step in range(4):

            @pl.when(c >= 1)
            def _():
                ag_step(c - 1, 0, step)
                ag_step(c - 1, 1, step)

            rs_step(c, 0, step)
            if step == 0:
                products(c, 1)
            rs_step(c, 1, step)
            if step == 0:
                pl.when(c >= 2)(lambda: finish(c - 2))
            if step == 1:

                @pl.when(c + 2 < CHUNKS)
                def _():
                    build(c + 2)
                    send_rows(c + 2)

            if step == 3:

                @pl.when(c + 1 < CHUNKS)
                def _():
                    take_rows(c + 1)
                    products(c + 1, 0)

        return carry

    lax.fori_loop(0, CHUNKS, turn, 0)

    stores = []

    def store(src, dst):
        stores.append(pltpu.make_async_copy(src, dst, out_sem.at[len(stores)]))
        stores[-1].start()

    def weight_grads(t, e):
        span = slice(e * exp_rows, (e + 1) * exp_rows)
        wgu_st[e, :, t * ff : (t + 1) * ff] = dot(
            rows[span, 0:width], act[t, span, strip:wide], 0, 0
        ).astype(BF)
        for u in range(2):
            store(
                wgu_st.at[e, :, pl.ds(t * ff + u * strip, strip)],
                wgu_out.at[e, :, pl.ds(u * ff + t * strip, strip)],
            )
        wdn_st[e, t * strip : (t + 1) * strip, :] = dot(
            act[t, span, 0:strip], rows[span, width : 2 * width], 0, 0
        ).astype(BF)
        at = pl.ds(t * strip, strip)
        store(wdn_st.at[e, at], wdn_out.at[e, at])

    def combine(chunk):
        for i in range(SPOTS):
            remote_only(chunk, i, lambda: back_arrival(chunk, i).wait_recv())
        came = r_recv[chunk, :, :, 0:width].reshape(SPOTS * block, width)
        outs = dot(gate_hi[chunk], came, 0, 0) + dot(gate_lo[chunk], came, 0, 0)
        came = r_recv[chunk, :, :, width : 2 * width].reshape(SPOTS * block, width)
        grads = dot(pick_c[chunk], came, 0, 0)
        if chunk > 0:
            outs, grads = fin[0:tok, 0:width] + outs, fin[0:tok, width : 2 * width] + grads
        return outs, grads

    last = CHUNKS - 1
    for i in range(SPOTS):
        dispatch(last, i).wait_send()
    for step in range(4):
        ag_step(last, 0, step)
        ag_step(last, 1, step)
        if step == 0:
            finish(last - 1)
        if step == 2:
            finish_pair(lax.rem(tp + 2, 4))
    finish_pair(lax.rem(tp + 1, 4))
    finish_pair(lax.rem(tp + 3, 4))
    ag_last(last, 0)
    ag_last(last, 1)
    finish_pair(lax.rem(tp, 4))
    for t in range(2):
        for e in range(2):
            weight_grads(t, e)

    r_recv[0, core] = x_send[0, core]
    for chunk in range(CHUNKS):
        outs, grads = combine(chunk)
        if chunk < last:
            fin[0:tok, 0:width] = outs
            fin[0:tok, width : 2 * width] = grads
    moe_out[...] = outs.astype(BF)
    tokens_grad[...] = grads.astype(BF)

    for chunk in range(CHUNKS):
        for t in range(2):
            for way in range(2):
                for step in range(4):
                    ag_copy(chunk, t, way, step).wait_send()
        for i in range(SPOTS):
            remote_only(chunk, i, lambda i=i, chunk=chunk: back(chunk, i).wait_send())
    for chunk in range(CHUNKS - 2, CHUNKS):
        for t in range(2):
            rs_drain(chunk, t)
    for copy in stores:
        copy.wait()


def hand_on(*refs):
    count = (len(refs) - 2) // 3
    came, left = refs[-2:]
    loads, stores = [], []
    for src, dst, mid in zip(refs[:count], refs[count : 2 * count], refs[2 * count : 3 * count]):
        pieces = src.shape[0] if len(src.shape) == 3 else 1
        for piece in range(pieces):
            views = [src, mid, dst]
            if pieces > 1:
                views = [view.at[piece] for view in views]
            loads.append(pltpu.make_async_copy(views[0], views[1], came.at[len(loads)]))
            stores.append(pltpu.make_async_copy(views[1], views[2], left.at[len(stores)]))
            loads[-1].start()
    for load, copy in zip(loads, stores):
        load.wait()
        copy.start()
    for copy in stores:
        copy.wait()


def body(tokens, out_grad, routes, gates, w_gu, w_dn):
    tok, width = tokens.shape
    top = routes.shape[1]
    routes, gates = routes.T, gates.T
    ff = w_dn.shape[1]
    n_ctx = SIDE * SIDE * CORES
    cap = 3 * tok * top // (4 * n_ctx)
    block = 2 * cap
    chunk_rows = SPOTS * block
    all_rows = CHUNKS * chunk_rows
    wide = 3 * ff // 2
    dma = pltpu.SemaphoreType.DMA
    any_space = pl.BlockSpec(memory_space=pl.ANY)
    vmem = pl.BlockSpec(memory_space=pltpu.VMEM)
    flops = 6 * all_rows * width * 3 * ff
    results = pl.pallas_call(
        kernel,
        out_shape=(
            jax.ShapeDtypeStruct((tok, width), BF),
            jax.ShapeDtypeStruct((tok, width), BF),
            jax.ShapeDtypeStruct(w_gu.shape, BF),
            jax.ShapeDtypeStruct(w_dn.shape, BF),
        ),
        in_specs=[any_space] * 6,
        out_specs=(vmem, vmem, any_space, any_space),
        scratch_shapes=[
            pltpu.VMEM(routes.shape, routes.dtype),
            pltpu.VMEM(gates.shape, gates.dtype),
            pltpu.VMEM((tok, 2 * width), BF),
            pltpu.VMEM((all_rows, tok), BF),
            pltpu.VMEM((all_rows, tok), F32),
            pltpu.VMEM((CHUNKS, chunk_rows, tok), BF),
            pltpu.VMEM((CHUNKS, chunk_rows, tok), BF),
            pltpu.VMEM((CHUNKS, chunk_rows, tok), BF),
            pltpu.VMEM((CHUNKS, SPOTS, block, 2 * width), BF),
            pltpu.VMEM((CHUNKS, SPOTS, block, 2 * width), BF),
            pltpu.VMEM((all_rows, 2 * width), BF),
            pltpu.VMEM(w_gu.shape, BF),
            pltpu.VMEM(w_dn.shape, BF),
            pltpu.VMEM((2, 2, chunk_rows, wide), F32),
            pltpu.VMEM((2, 2, 2, 4, block, wide), BF),
            pltpu.VMEM((CHUNKS, 2, 2, 4, block, wide), BF),
            pltpu.VMEM((2, all_rows, wide), BF),
            pltpu.VMEM((chunk_rows, 2 * width), F32),
            pltpu.VMEM((CHUNKS, SPOTS, block, 2 * width), BF),
            pltpu.VMEM(w_gu.shape, BF),
            pltpu.VMEM(w_dn.shape, BF),
            dma((9,)),
            dma((CHUNKS, SPOTS)),
            dma((CHUNKS, SPOTS)),
            dma((CHUNKS, 2, 2, 4)),
            dma((CHUNKS, 2, 2, 4)),
            dma((CHUNKS, 2, 2, 4)),
            dma((CHUNKS, 2, 2, 4)),
            dma((CHUNKS, SPOTS)),
            dma((CHUNKS, SPOTS)),
            dma((12,)),
        ],
        compiler_params=pltpu.CompilerParams(
            collective_id=0, has_side_effects=True, vmem_limit_bytes=60 * 1024 * 1024
        ),
        cost_estimate=pl.CostEstimate(flops=flops, bytes_accessed=10 << 20, transcendentals=0),
        name="moe",
    )(tokens, out_grad, routes, gates, w_gu, w_dn)
    return pl.pallas_call(
        hand_on,
        out_shape=tuple(jax.ShapeDtypeStruct(r.shape, r.dtype) for r in results),
        in_specs=[any_space] * 4,
        out_specs=(any_space,) * 4,
        scratch_shapes=[pltpu.VMEM(r.shape, r.dtype) for r in results] + [dma((6,)), dma((6,))],
        compiler_params=pltpu.CompilerParams(vmem_limit_bytes=60 * 1024 * 1024),
        name="hand_on",
    )(*results)


def solution(mesh):
    return jax.shard_map(
        body,
        mesh=mesh,
        in_specs=(
            P("ctx", "tp"),
            P("ctx", "tp"),
            P("ctx", None),
            P("ctx", None),
            P("ctx", "tp", None),
            P("ctx", None, "tp"),
        ),
        out_specs=(P("ctx", "tp"), P("ctx", "tp"), P("ctx", "tp", None), P("ctx", None, "tp")),
        check_vma=False,
    )
```

```python
import functools

import jax
import jax.numpy as jnp
from jax import lax
from jax.experimental import pallas as pl
from jax.experimental.pallas import tpu as pltpu
from jax.sharding import PartitionSpec as P

BF = jnp.bfloat16
F32 = jnp.float32
MESH = pl.DeviceIdType.MESH
SIDE = 4
CORES = 2
CHUNKS = 4
SPOTS = 8
RING = 8

OFFSETS = (
    ((0, 0), (1, 0), (3, 0), (0, 1)),
    ((2, 0), (0, 2), (2, 2), (3, 3)),
    ((2, 1), (2, 3), (1, 2), (3, 2)),
    ((0, 3), (1, 1), (3, 1), (1, 3)),
)


def dot(a, b, ca=1, cb=0):
    return lax.dot_general(a, b, (((ca,), (cb,)), ((), ())), preferred_element_type=F32)


def pick(chunk, values):
    result = values[-1]
    for index in range(len(values) - 2, -1, -1):
        result = jnp.where(chunk == index, values[index], result)
    return result


def kernel(
    tokens, out_grad, routes_in, gates_in, w_gu, w_dn,
    moe_out, tokens_grad, wgu_out, wdn_out,
    routes, gates, tg, pick_all, gate_all, pick_c, gate_hi, gate_lo,
    x_send, x_recv, rows, wgu, wdn, part, rs_send, rs_recv, act, fin, acc, r_recv, wgu_st, wdn_st,
    ld_sem, xs_sem, xr_sem, rss_sem, rsr_sem, ags_sem, agr_sem, rts_sem, rtr_sem, out_sem,
):
    ctx = lax.axis_index("ctx")
    tp = lax.axis_index("tp")
    n_ctx = SIDE * SIDE * CORES
    core = lax.rem(ctx, CORES)
    my_y = lax.rem(ctx // CORES, SIDE)
    my_x = ctx // (CORES * SIDE)
    up = lax.rem(tp + 1, RING)
    down = lax.rem(tp + RING - 1, RING)
    top, tok = routes_in.shape
    width = tokens.shape[1]
    ff = wdn.shape[1]
    cap = x_send.shape[2] // 2
    block = 2 * cap
    exp_rows = n_ctx * cap
    half_rows = SPOTS * cap
    strip = ff // 2
    wide = 3 * strip
    cuts = (2 * block // 3, block // 3)
    experts = 2 * n_ctx

    barrier = pltpu.get_barrier_semaphore()

    def greet(i, carry):
        pl.semaphore_signal(
            barrier, inc=1, device_id=(lax.rem(ctx + 1 + i, n_ctx), tp), device_id_type=MESH
        )
        return carry

    lax.fori_loop(0, n_ctx - 1, greet, 0)
    pl.semaphore_signal(barrier, inc=1, device_id=(ctx, up), device_id_type=MESH)
    pl.semaphore_signal(barrier, inc=1, device_id=(ctx, down), device_id_type=MESH)

    loads = [
        pltpu.make_async_copy(tokens, tg.at[:, pl.ds(0, width)], ld_sem.at[0]),
        pltpu.make_async_copy(out_grad, tg.at[:, pl.ds(width, width)], ld_sem.at[1]),
        pltpu.make_async_copy(w_dn, wdn, ld_sem.at[2]),
    ]
    for t in range(2):
        for u in range(2):
            loads.append(
                pltpu.make_async_copy(
                    w_gu.at[:, :, pl.ds(u * ff + t * strip, strip)],
                    wgu.at[:, :, pl.ds(t * ff + u * strip, strip)],
                    ld_sem.at[3 + 2 * t + u],
                )
            )
    tables = [
        pltpu.make_async_copy(routes_in, routes, ld_sem.at[7]),
        pltpu.make_async_copy(gates_in, gates, ld_sem.at[8]),
    ]
    for load in tables + loads:
        load.start()
    for load in tables:
        load.wait()

    ids = lax.broadcasted_iota(jnp.int32, (experts, tok), 0)
    named = jnp.zeros((experts, tok), F32)
    gate_t = jnp.zeros((experts, tok), F32)
    for k in range(top):
        hit = routes[k : k + 1, :] == ids
        named = named + jnp.where(hit, 1.0, 0.0)
        gate_t = gate_t + jnp.where(hit, gates[k : k + 1, :], 0.0)
    before = (
        lax.broadcasted_iota(jnp.int32, (tok, tok), 0)
        < lax.broadcasted_iota(jnp.int32, (tok, tok), 1)
    )
    earlier = dot(named.astype(BF), jnp.where(before, 1.0, 0.0).astype(BF))
    slot = jnp.where(named > 0.5, earlier, -1.0)
    group = 8
    for g in range(experts // group):
        part_slot = slot[g * group : (g + 1) * group][:, None, :]
        part_gate = gate_t[g * group : (g + 1) * group][:, None, :]
        wanted = lax.broadcasted_iota(jnp.int32, (group, cap, tok), 1).astype(F32)
        owned = part_slot == wanted
        span = pl.ds(g * group * cap, group * cap)
        pick_all[span, :] = jnp.where(owned, 1.0, 0.0).reshape(group * cap, tok).astype(BF)
        gate_all[span, :] = jnp.where(owned, part_gate, 0.0).reshape(group * cap, tok)
    loads[0].wait()
    loads[1].wait()

    def peer(chunk, q, sign):
        if isinstance(q, int):
            dx = pick(chunk, [OFFSETS[c][q][0] for c in range(CHUNKS)])
            dy = pick(chunk, [OFFSETS[c][q][1] for c in range(CHUNKS)])
        else:
            dx = pick(q, [offset[0] for offset in OFFSETS[chunk]])
            dy = pick(q, [offset[1] for offset in OFFSETS[chunk]])
        px = lax.rem(my_x + sign * dx + SIDE, SIDE)
        py = lax.rem(my_y + sign * dy + SIDE, SIDE)
        return (px * SIDE + py) * CORES

    def spot(q):
        return 2 * ((q - core + 4) % 4) + core

    def origin(chunk, k, b):
        if isinstance(k, int):
            return peer(chunk, (k + b) % 4, 1) + b
        return peer(chunk, lax.rem(k + b, 4), 1) + b

    def dispatch(chunk, i):
        q, b = i // 2, i % 2
        return pltpu.make_async_remote_copy(
            src_ref=x_send.at[chunk, i], dst_ref=x_recv.at[chunk, spot(q)],
            send_sem=xs_sem.at[chunk, i], recv_sem=xr_sem.at[chunk, spot(q)],
            device_id=(peer(chunk, q, -1) + b, tp), device_id_type=MESH,
        )

    def arrival(chunk, i):
        return pltpu.make_async_remote_copy(
            src_ref=x_send.at[chunk, i], dst_ref=x_recv.at[chunk, i],
            send_sem=xs_sem.at[chunk, i], recv_sem=xr_sem.at[chunk, i],
            device_id=(origin(chunk, i // 2, i % 2), tp), device_id_type=MESH,
        )

    def back(chunk, b, k):
        q = (k + b) % 4 if isinstance(k, int) else lax.rem(k + b, 4)
        return pltpu.make_async_remote_copy(
            src_ref=x_send.at[chunk, 2 * k + b], dst_ref=r_recv.at[chunk, 2 * q + core],
            send_sem=rts_sem.at[chunk, 2 * k + b], recv_sem=rtr_sem.at[chunk, 2 * q + core],
            device_id=(origin(chunk, k, b), tp), device_id_type=MESH,
        )

    def back_arrival(chunk, i):
        return pltpu.make_async_remote_copy(
            src_ref=x_send.at[chunk, i], dst_ref=r_recv.at[chunk, i],
            send_sem=rts_sem.at[chunk, i], recv_sem=rtr_sem.at[chunk, i],
            device_id=(peer(chunk, i // 2, -1) + i % 2, tp), device_id_type=MESH,
        )

    self_spot = 7 * core

    def others(chunk, i, own, act_on):
        if i in own:
            pl.when(jnp.logical_or(chunk != 0, core != own.index(i)))(act_on)
        else:
            act_on()

    LISTED, HELD = (0, 1), (0, 7)

    def build(chunk):
        for i in range(SPOTS):
            dest = peer(chunk, i // 2, -1) + i % 2
            span = pl.ds(pl.multiple_of(dest * block, block), block)
            here = pl.ds(i * block, block)
            pick_c[chunk, here, :] = pick_all[span, :]
            weights = gate_all[span, :]
            high = weights.astype(BF)
            gate_hi[chunk, here, :] = high
            gate_lo[chunk, here, :] = (weights - high.astype(F32)).astype(BF)
            fin[pl.ds(i * block, block), 0:1] = jnp.sum(weights, axis=1, keepdims=True)
        chosen = dot(pick_c[chunk], tg[:, 0:width])
        x_send[chunk, :, :, 0:width] = chosen.astype(BF).reshape(SPOTS, block, width)
        chosen = dot(pick_c[chunk], tg[:, width : 2 * width]) * fin[:, 0:1]
        x_send[chunk, :, :, width : 2 * width] = chosen.astype(BF).reshape(SPOTS, block, width)

    def send_rows(chunk):
        for i in range(SPOTS):
            others(chunk, i, LISTED, lambda i=i: dispatch(chunk, i).start())

    def take_rows(chunk):
        for i in range(SPOTS):
            others(chunk, i, HELD, lambda i=i: arrival(chunk, i).wait_recv())
        for pair in range(SPOTS // 2):
            first = x_recv[chunk, 2 * pair].astype(F32)
            second = x_recv[chunk, 2 * pair + 1].astype(F32)
            for e in range(2):
                both = jnp.concatenate(
                    [first[e * cap : (e + 1) * cap], second[e * cap : (e + 1) * cap]], axis=0
                )
                start = e * exp_rows + chunk * half_rows + pair * block
                rows[pl.ds(pl.multiple_of(start, 16), block), :] = both.astype(BF)

    def products(chunk, t):
        side = lax.rem(chunk, 2)
        for e in range(2):
            span = pl.ds(pl.multiple_of(e * exp_rows + chunk * half_rows, 16), half_rows)
            out = pl.ds(e * half_rows, half_rows)
            left, grads = rows[span, 0:width], rows[span, width : 2 * width]
            part[side, t, out, 0 : 2 * strip] = dot(left, wgu[e, :, t * ff : (t + 1) * ff])
            part[side, t, out, 2 * strip : wide] = dot(
                grads, wdn[e, t * strip : (t + 1) * strip, :], 1, 1
            )

    def own_rows(owner):
        return pl.ds(pl.multiple_of(owner * block, block), block)

    def cut(t, way):
        return (0, cuts[t]) if way == 0 else (cuts[t], block - cuts[t])

    def some(start, t, way):
        first, count = cut(t, way)
        return pl.ds(pl.multiple_of(start + first, 16), count)

    def rs_copy(chunk, t, way, step):
        side = lax.rem(chunk, 2)
        src, dst = rs_send.at[side, t, way, step], rs_recv.at[chunk, t, way, step]
        if step == 0:
            src, dst = src.at[pl.ds(*cut(t, way))], dst.at[pl.ds(*cut(t, way))]
        return pltpu.make_async_remote_copy(
            src_ref=src, dst_ref=dst,
            send_sem=rss_sem.at[chunk, t, way, step], recv_sem=rsr_sem.at[chunk, t, way, step],
            device_id=(ctx, (up, down)[way]), device_id_type=MESH,
        )

    def rs_drain(chunk, t):
        for way in range(2):
            for step in range(4):
                rs_copy(chunk, t, way, step).wait_send()

    def rs_step(chunk, t, step):
        side = lax.rem(chunk, 2)
        if step == 0:
            pl.when(chunk >= 2)(lambda: rs_drain(chunk - 2, t))
        for way in range(2):
            owner = lax.rem(tp + (4 - step if way == 0 else 4 + step), RING)
            if step > 0:
                rs_copy(chunk, t, way, step - 1).wait_recv()
            for w in range(2):
                if step == 0 and w != way:
                    continue
                value = part[side, t, some(owner * block, t, w), :]
                here = pl.ds(*cut(t, w))
                if step > 1 or (step == 1 and w == way):
                    value = value + rs_recv[chunk, t, way, step - 1, here, :].astype(F32)
                rs_send[side, t, way, step, here, :] = value.astype(BF)
            rs_copy(chunk, t, way, step).start()

    def act_start(chunk, owner):
        return (owner // 4) * exp_rows + chunk * half_rows + lax.rem(owner, 4) * block

    def act_rows(chunk, owner):
        return pl.ds(pl.multiple_of(act_start(chunk, owner), 16), block)

    def rs_last(chunk, t):
        side = lax.rem(chunk, 2)
        for way in range(2):
            rs_copy(chunk, t, way, 3).wait_recv()

        def total(s):
            cols = slice(s * strip, (s + 1) * strip)
            value = part[side, t, own_rows(tp), cols]
            for way in range(2):
                value = value + rs_recv[chunk, t, way, 3, :, cols].astype(F32)
            return value

        out = act_rows(chunk, tp)
        gate, upper, grad = total(0), total(1), total(2)
        sigma = jax.nn.sigmoid(gate)
        silu = gate * sigma
        act[t, out, 0:strip] = (silu * upper).astype(BF)
        act[t, out, strip : 2 * strip] = (
            grad * upper * sigma * (1.0 + gate * (1.0 - sigma))
        ).astype(BF)
        act[t, out, 2 * strip : wide] = (grad * silu).astype(BF)

    def ag_move(chunk, t, way, step, owner):
        start = act_start(chunk, lax.rem(owner, RING))
        ref = act.at[t, pl.ds(pl.multiple_of(start, 16), block) if step < 3 else some(start, t, way)]
        return pltpu.make_async_remote_copy(
            src_ref=ref, dst_ref=ref,
            send_sem=ags_sem.at[chunk, t, way, step], recv_sem=agr_sem.at[chunk, t, way, step],
            device_id=(ctx, (up, down)[way]), device_id_type=MESH,
        )

    def ag_copy(chunk, t, way, step):
        return ag_move(chunk, t, way, step, tp + (RING - step if way == 0 else step))

    def ag_arrival(chunk, t, way, step):
        return ag_move(chunk, t, way, step, tp + (RING - step - 1 if way == 0 else step + 1))

    def ag_step(chunk, t, step):
        if step == 0:
            rs_last(chunk, t)
        for way in range(2):
            if step > 0:
                ag_arrival(chunk, t, way, step - 1).wait_recv()
            ag_copy(chunk, t, way, step).start()

    def ag_last(chunk, t):
        for way in range(2):
            ag_arrival(chunk, t, way, 3).wait_recv()

    def rows_out(e, span):
        outs = dot(act[0, span, 0:strip], wdn[e, 0:strip, :]) + dot(
            act[1, span, 0:strip], wdn[e, strip : 2 * strip, :]
        )
        grads = dot(act[0, span, strip:wide], wgu[e, :, 0:ff], 1, 1) + dot(
            act[1, span, strip:wide], wgu[e, :, ff : 2 * ff], 1, 1
        )
        return outs, grads

    def pair_rows(q, e):
        start = e * exp_rows + (CHUNKS - 1) * half_rows + q * block
        out = pl.ds(pl.multiple_of(e * block, 16), block)
        outs, grads = rows_out(e, pl.ds(pl.multiple_of(start, 16), block))
        fin[out, 0:width] = outs
        fin[out, width : 2 * width] = grads

    def send_pair(q):
        chunk = CHUNKS - 1
        for b in range(2):
            at = b * cap
            both = jnp.concatenate([fin[at : at + cap, :], fin[block + at : block + at + cap, :]], axis=0)
            x_send[chunk, 2 * q + b] = both.astype(BF)
            back(chunk, b, q).start()

    def finish(chunk):
        ag_last(chunk, 0)
        ag_last(chunk, 1)
        for i in range(SPOTS):
            others(chunk, i, LISTED, lambda i=i: dispatch(chunk, i).wait_send())
        for e in range(2):
            span = pl.ds(pl.multiple_of(e * exp_rows + chunk * half_rows, 16), half_rows)
            out = pl.ds(e * half_rows, half_rows)
            outs, grads = rows_out(e, span)
            fin[out, 0:width] = outs
            fin[out, width : 2 * width] = grads
        for i in range(SPOTS):
            both = jnp.concatenate(
                [
                    fin[i * cap : (i + 1) * cap, :],
                    fin[half_rows + i * cap : half_rows + (i + 1) * cap, :],
                ],
                axis=0,
            )
            x_send[chunk, i] = both.astype(BF)
            others(chunk, i, HELD, lambda i=i: back(chunk, i % 2, i // 2).start())

    build(0)
    pl.semaphore_wait(barrier, n_ctx + 1)
    send_rows(0)
    x_recv[0, self_spot] = x_send[0, core]
    build(1)
    for load in loads[2:]:
        load.wait()
    take_rows(0)
    send_rows(1)
    products(0, 0)

    def turn(c, carry):
        for step in range(4):

            @pl.when(c >= 1)
            def _():
                ag_step(c - 1, 0, step)
                ag_step(c - 1, 1, step)

            rs_step(c, 0, step)
            if step == 0:
                products(c, 1)
            rs_step(c, 1, step)
            if step == 0:
                pl.when(c >= 2)(lambda: finish(c - 2))
            if step == 1:

                @pl.when(c + 2 < CHUNKS)
                def _():
                    build(c + 2)
                    send_rows(c + 2)

            if step == 3:

                @pl.when(c + 1 < CHUNKS)
                def _():
                    take_rows(c + 1)
                    products(c + 1, 0)

        return carry

    lax.fori_loop(0, CHUNKS, turn, 0)

    stores = []

    def store(src, dst):
        stores.append(pltpu.make_async_copy(src, dst, out_sem.at[len(stores)]))
        stores[-1].start()

    def weight_grads(t, e):
        span = slice(e * exp_rows, (e + 1) * exp_rows)
        wgu_st[e, :, t * ff : (t + 1) * ff] = dot(
            rows[span, 0:width], act[t, span, strip:wide], 0, 0
        ).astype(BF)
        for u in range(2):
            store(
                wgu_st.at[e, :, pl.ds(t * ff + u * strip, strip)],
                wgu_out.at[e, :, pl.ds(u * ff + t * strip, strip)],
            )
        wdn_st[e, t * strip : (t + 1) * strip, :] = dot(
            act[t, span, 0:strip], rows[span, width : 2 * width], 0, 0
        ).astype(BF)
        at = pl.ds(t * strip, strip)
        store(wdn_st.at[e, at], wdn_out.at[e, at])

    def combine(chunk):
        for i in range(SPOTS):
            others(chunk, i, LISTED, lambda: back_arrival(chunk, i).wait_recv())
        came = r_recv[chunk, :, :, 0:width].reshape(SPOTS * block, width)
        outs = dot(gate_hi[chunk], came, 0, 0) + dot(gate_lo[chunk], came, 0, 0)
        came = r_recv[chunk, :, :, width : 2 * width].reshape(SPOTS * block, width)
        grads = dot(pick_c[chunk], came, 0, 0)
        if chunk > 0:
            outs, grads = acc[:, 0:width] + outs, acc[:, width : 2 * width] + grads
        if chunk < CHUNKS - 1:
            acc[:, 0:width] = outs
            acc[:, width : 2 * width] = grads
        return outs, grads

    last = CHUNKS - 1
    for i in range(SPOTS):
        dispatch(last, i).wait_send()
    def finish_pair(q):
        pair_rows(q, 0)
        pair_rows(q, 1)
        send_pair(q)

    for step in range(4):
        ag_step(last, 0, step)
        ag_step(last, 1, step)
        if step == 0:
            finish(last - 1)
            r_recv[0, core] = x_send[0, self_spot]
        if step == 1:
            combine(0)
            combine(1)
        if step == 2:
            finish_pair(lax.rem(tp + 2, 4))
    finish_pair(lax.rem(tp + 1, 4))
    finish_pair(lax.rem(tp + 3, 4))
    pair_rows(lax.rem(tp, 4), tp // 4)
    ag_last(last, 0)
    ag_last(last, 1)
    pair_rows(lax.rem(tp, 4), 1 - tp // 4)
    send_pair(lax.rem(tp, 4))
    for t in range(2):
        for e in range(2):
            weight_grads(t, e)

    combine(2)
    outs, grads = combine(3)
    moe_out[...] = outs.astype(BF)
    tokens_grad[...] = grads.astype(BF)

    for chunk in range(CHUNKS):
        for t in range(2):
            for way in range(2):
                for step in range(4):
                    ag_copy(chunk, t, way, step).wait_send()
        for i in range(SPOTS):
            others(chunk, i, HELD, lambda i=i, chunk=chunk: back(chunk, i % 2, i // 2).wait_send())
    for chunk in range(CHUNKS - 2, CHUNKS):
        for t in range(2):
            rs_drain(chunk, t)
    for copy in stores:
        copy.wait()


def hand_on(*refs):
    count = (len(refs) - 2) // 3
    came, left = refs[-2:]
    loads, stores = [], []
    for src, dst, mid in zip(refs[:count], refs[count : 2 * count], refs[2 * count : 3 * count]):
        pieces = src.shape[0] if len(src.shape) == 3 else 1
        for piece in range(pieces):
            views = [src, mid, dst]
            if pieces > 1:
                views = [view.at[piece] for view in views]
            loads.append(pltpu.make_async_copy(views[0], views[1], came.at[len(loads)]))
            stores.append(pltpu.make_async_copy(views[1], views[2], left.at[len(stores)]))
            loads[-1].start()
    for load, copy in zip(loads, stores):
        load.wait()
        copy.start()
    for copy in stores:
        copy.wait()


def body(tokens, out_grad, routes, gates, w_gu, w_dn):
    tok, width = tokens.shape
    top = routes.shape[1]
    routes, gates = routes.T, gates.T
    ff = w_dn.shape[1]
    n_ctx = SIDE * SIDE * CORES
    cap = 3 * tok * top // (4 * n_ctx)
    block = 2 * cap
    chunk_rows = SPOTS * block
    all_rows = CHUNKS * chunk_rows
    wide = 3 * ff // 2
    dma = pltpu.SemaphoreType.DMA
    any_space = pl.BlockSpec(memory_space=pl.ANY)
    vmem = pl.BlockSpec(memory_space=pltpu.VMEM)
    flops = 6 * all_rows * width * 3 * ff
    results = pl.pallas_call(
        kernel,
        out_shape=(
            jax.ShapeDtypeStruct((tok, width), BF),
            jax.ShapeDtypeStruct((tok, width), BF),
            jax.ShapeDtypeStruct(w_gu.shape, BF),
            jax.ShapeDtypeStruct(w_dn.shape, BF),
        ),
        in_specs=[any_space] * 6,
        out_specs=(vmem, vmem, any_space, any_space),
        scratch_shapes=[
            pltpu.VMEM(routes.shape, routes.dtype),
            pltpu.VMEM(gates.shape, gates.dtype),
            pltpu.VMEM((tok, 2 * width), BF),
            pltpu.VMEM((all_rows, tok), BF),
            pltpu.VMEM((all_rows, tok), F32),
            pltpu.VMEM((CHUNKS, chunk_rows, tok), BF),
            pltpu.VMEM((CHUNKS, chunk_rows, tok), BF),
            pltpu.VMEM((CHUNKS, chunk_rows, tok), BF),
            pltpu.VMEM((CHUNKS, SPOTS, block, 2 * width), BF),
            pltpu.VMEM((CHUNKS, SPOTS, block, 2 * width), BF),
            pltpu.VMEM((all_rows, 2 * width), BF),
            pltpu.VMEM(w_gu.shape, BF),
            pltpu.VMEM(w_dn.shape, BF),
            pltpu.VMEM((2, 2, chunk_rows, wide), F32),
            pltpu.VMEM((2, 2, 2, 4, block, wide), BF),
            pltpu.VMEM((CHUNKS, 2, 2, 4, block, wide), BF),
            pltpu.VMEM((2, all_rows, wide), BF),
            pltpu.VMEM((chunk_rows, 2 * width), F32),
            pltpu.VMEM((tok, 2 * width), F32),
            pltpu.VMEM((CHUNKS, SPOTS, block, 2 * width), BF),
            pltpu.VMEM(w_gu.shape, BF),
            pltpu.VMEM(w_dn.shape, BF),
            dma((9,)),
            dma((CHUNKS, SPOTS)),
            dma((CHUNKS, SPOTS)),
            dma((CHUNKS, 2, 2, 4)),
            dma((CHUNKS, 2, 2, 4)),
            dma((CHUNKS, 2, 2, 4)),
            dma((CHUNKS, 2, 2, 4)),
            dma((CHUNKS, SPOTS)),
            dma((CHUNKS, SPOTS)),
            dma((12,)),
        ],
        compiler_params=pltpu.CompilerParams(
            collective_id=0, has_side_effects=True, vmem_limit_bytes=60 * 1024 * 1024
        ),
        cost_estimate=pl.CostEstimate(flops=flops, bytes_accessed=10 << 20, transcendentals=0),
        name="moe",
    )(tokens, out_grad, routes, gates, w_gu, w_dn)
    return pl.pallas_call(
        hand_on,
        out_shape=tuple(jax.ShapeDtypeStruct(r.shape, r.dtype) for r in results),
        in_specs=[any_space] * 4,
        out_specs=(any_space,) * 4,
        scratch_shapes=[pltpu.VMEM(r.shape, r.dtype) for r in results] + [dma((6,)), dma((6,))],
        compiler_params=pltpu.CompilerParams(vmem_limit_bytes=60 * 1024 * 1024),
        name="hand_on",
    )(*results)


def solution(mesh):
    return jax.shard_map(
        body,
        mesh=mesh,
        in_specs=(
            P("ctx", "tp"),
            P("ctx", "tp"),
            P("ctx", None),
            P("ctx", None),
            P("ctx", "tp", None),
            P("ctx", None, "tp"),
        ),
        out_specs=(P("ctx", "tp"), P("ctx", "tp"), P("ctx", "tp", None), P("ctx", None, "tp")),
        check_vma=False,
    )
```

```python
import functools

import jax
import jax.numpy as jnp
from jax import lax
from jax.experimental import pallas as pl
from jax.experimental.pallas import tpu as pltpu
from jax.sharding import PartitionSpec as P

BF = jnp.bfloat16
F32 = jnp.float32
MESH = pl.DeviceIdType.MESH
SIDE = 4
CORES = 2
CHUNKS = 4
SPOTS = 8
RING = 8

OFFSETS = (
    ((0, 0), (1, 0), (3, 0), (0, 1)),
    ((2, 2), (2, 1), (2, 3), (1, 2)),
    ((2, 0), (0, 2), (3, 2), (1, 3)),
    ((0, 3), (1, 1), (3, 3), (3, 1)),
)


def dot(a, b, ca=1, cb=0):
    return lax.dot_general(a, b, (((ca,), (cb,)), ((), ())), preferred_element_type=F32)


def pick(chunk, values):
    result = values[-1]
    for index in range(len(values) - 2, -1, -1):
        result = jnp.where(chunk == index, values[index], result)
    return result


def kernel(
    tokens, out_grad, routes_in, gates_in, w_gu, w_dn,
    moe_out, tokens_grad, wgu_out, wdn_out,
    routes, gates, tg, pick_all, gate_all, pick_c, gate_hi, gate_lo,
    x_send, x_recv, rows, wgu, wdn, part, rs_send, rs_recv, act, fin, acc, r_recv, wgu_st, wdn_st, gu_sum, dn_sum,
    ld_sem, xs_sem, xr_sem, rss_sem, rsr_sem, ags_sem, agr_sem, rts_sem, rtr_sem, out_sem,
):
    ctx = lax.axis_index("ctx")
    tp = lax.axis_index("tp")
    n_ctx = SIDE * SIDE * CORES
    core = lax.rem(ctx, CORES)
    my_y = lax.rem(ctx // CORES, SIDE)
    my_x = ctx // (CORES * SIDE)
    up = lax.rem(tp + 1, RING)
    down = lax.rem(tp + RING - 1, RING)
    top, tok = routes_in.shape
    width = tokens.shape[1]
    ff = wdn.shape[1]
    cap = x_send.shape[2] // 2
    block = 2 * cap
    exp_rows = n_ctx * cap
    half_rows = SPOTS * cap
    strip = ff // 2
    wide = 3 * strip
    cuts = (2 * block // 3, block // 3)
    experts = 2 * n_ctx

    barrier = pltpu.get_barrier_semaphore()

    def greet(i, carry):
        pl.semaphore_signal(
            barrier, inc=1, device_id=(lax.rem(ctx + 1 + i, n_ctx), tp), device_id_type=MESH
        )
        return carry

    lax.fori_loop(0, n_ctx - 1, greet, 0)
    pl.semaphore_signal(barrier, inc=1, device_id=(ctx, up), device_id_type=MESH)
    pl.semaphore_signal(barrier, inc=1, device_id=(ctx, down), device_id_type=MESH)

    loads = [
        pltpu.make_async_copy(tokens, tg.at[:, pl.ds(0, width)], ld_sem.at[0]),
        pltpu.make_async_copy(out_grad, tg.at[:, pl.ds(width, width)], ld_sem.at[1]),
        pltpu.make_async_copy(w_dn, wdn, ld_sem.at[2]),
    ]
    for t in range(2):
        for u in range(2):
            loads.append(
                pltpu.make_async_copy(
                    w_gu.at[:, :, pl.ds(u * ff + t * strip, strip)],
                    wgu.at[:, :, pl.ds(t * ff + u * strip, strip)],
                    ld_sem.at[3 + 2 * t + u],
                )
            )
    tables = [
        pltpu.make_async_copy(routes_in, routes, ld_sem.at[7]),
        pltpu.make_async_copy(gates_in, gates, ld_sem.at[8]),
    ]
    for load in tables + loads:
        load.start()
    for load in tables:
        load.wait()

    ids = lax.broadcasted_iota(jnp.int32, (experts, tok), 0)
    named = jnp.zeros((experts, tok), F32)
    gate_t = jnp.zeros((experts, tok), F32)
    for k in range(top):
        hit = routes[k : k + 1, :] == ids
        named = named + jnp.where(hit, 1.0, 0.0)
        gate_t = gate_t + jnp.where(hit, gates[k : k + 1, :], 0.0)
    before = (
        lax.broadcasted_iota(jnp.int32, (tok, tok), 0)
        < lax.broadcasted_iota(jnp.int32, (tok, tok), 1)
    )
    earlier = dot(named.astype(BF), jnp.where(before, 1.0, 0.0).astype(BF))
    slot = jnp.where(named > 0.5, earlier, -1.0)
    group = 8
    for g in range(experts // group):
        part_slot = slot[g * group : (g + 1) * group][:, None, :]
        part_gate = gate_t[g * group : (g + 1) * group][:, None, :]
        wanted = lax.broadcasted_iota(jnp.int32, (group, cap, tok), 1).astype(F32)
        owned = part_slot == wanted
        span = pl.ds(g * group * cap, group * cap)
        pick_all[span, :] = jnp.where(owned, 1.0, 0.0).reshape(group * cap, tok).astype(BF)
        gate_all[span, :] = jnp.where(owned, part_gate, 0.0).reshape(group * cap, tok)
    loads[0].wait()
    loads[1].wait()

    def peer(chunk, q, sign):
        if isinstance(q, int):
            dx = pick(chunk, [OFFSETS[c][q][0] for c in range(CHUNKS)])
            dy = pick(chunk, [OFFSETS[c][q][1] for c in range(CHUNKS)])
        else:
            dx = pick(q, [offset[0] for offset in OFFSETS[chunk]])
            dy = pick(q, [offset[1] for offset in OFFSETS[chunk]])
        px = lax.rem(my_x + sign * dx + SIDE, SIDE)
        py = lax.rem(my_y + sign * dy + SIDE, SIDE)
        return (px * SIDE + py) * CORES

    def spot(q):
        return 2 * ((q - core + 4) % 4) + core

    def origin(chunk, k, b):
        if isinstance(k, int):
            return peer(chunk, (k + b) % 4, 1) + b
        return peer(chunk, lax.rem(k + b, 4), 1) + b

    def dispatch(chunk, i):
        q, b = i // 2, i % 2
        return pltpu.make_async_remote_copy(
            src_ref=x_send.at[chunk, i], dst_ref=x_recv.at[chunk, spot(q)],
            send_sem=xs_sem.at[chunk, i], recv_sem=xr_sem.at[chunk, spot(q)],
            device_id=(peer(chunk, q, -1) + b, tp), device_id_type=MESH,
        )

    def arrival(chunk, i):
        return pltpu.make_async_remote_copy(
            src_ref=x_send.at[chunk, i], dst_ref=x_recv.at[chunk, i],
            send_sem=xs_sem.at[chunk, i], recv_sem=xr_sem.at[chunk, i],
            device_id=(origin(chunk, i // 2, i % 2), tp), device_id_type=MESH,
        )

    def back(chunk, b, k):
        q = (k + b) % 4 if isinstance(k, int) else lax.rem(k + b, 4)
        return pltpu.make_async_remote_copy(
            src_ref=x_send.at[chunk, 2 * k + b], dst_ref=r_recv.at[chunk, 2 * q + core],
            send_sem=rts_sem.at[chunk, 2 * k + b], recv_sem=rtr_sem.at[chunk, 2 * q + core],
            device_id=(origin(chunk, k, b), tp), device_id_type=MESH,
        )

    def back_arrival(chunk, i):
        return pltpu.make_async_remote_copy(
            src_ref=x_send.at[chunk, i], dst_ref=r_recv.at[chunk, i],
            send_sem=rts_sem.at[chunk, i], recv_sem=rtr_sem.at[chunk, i],
            device_id=(peer(chunk, i // 2, -1) + i % 2, tp), device_id_type=MESH,
        )

    self_spot = 7 * core

    def others(chunk, i, own, act_on):
        if i in own:
            pl.when(jnp.logical_or(chunk != 0, core != own.index(i)))(act_on)
        else:
            act_on()

    LISTED, HELD = (0, 1), (0, 7)

    def build(chunk):
        for i in range(SPOTS):
            dest = peer(chunk, i // 2, -1) + i % 2
            span = pl.ds(pl.multiple_of(dest * block, block), block)
            here = pl.ds(i * block, block)
            pick_c[chunk, here, :] = pick_all[span, :]
            weights = gate_all[span, :]
            high = weights.astype(BF)
            gate_hi[chunk, here, :] = high
            gate_lo[chunk, here, :] = (weights - high.astype(F32)).astype(BF)
            fin[pl.ds(i * block, block), 0:1] = jnp.sum(weights, axis=1, keepdims=True)
        chosen = dot(pick_c[chunk], tg[:, 0:width])
        x_send[chunk, :, :, 0:width] = chosen.astype(BF).reshape(SPOTS, block, width)
        chosen = dot(pick_c[chunk], tg[:, width : 2 * width]) * fin[:, 0:1]
        x_send[chunk, :, :, width : 2 * width] = chosen.astype(BF).reshape(SPOTS, block, width)

    def send_rows(chunk):
        for i in range(SPOTS):
            others(chunk, i, LISTED, lambda i=i: dispatch(chunk, i).start())

    def take_rows(chunk):
        for i in range(SPOTS):
            others(chunk, i, HELD, lambda i=i: arrival(chunk, i).wait_recv())
        for pair in range(SPOTS // 2):
            first = x_recv[chunk, 2 * pair].astype(F32)
            second = x_recv[chunk, 2 * pair + 1].astype(F32)
            for e in range(2):
                both = jnp.concatenate(
                    [first[e * cap : (e + 1) * cap], second[e * cap : (e + 1) * cap]], axis=0
                )
                start = e * exp_rows + chunk * half_rows + pair * block
                rows[pl.ds(pl.multiple_of(start, 16), block), :] = both.astype(BF)

    def products(chunk, t):
        side = lax.rem(chunk, 2)
        for e in range(2):
            span = pl.ds(pl.multiple_of(e * exp_rows + chunk * half_rows, 16), half_rows)
            out = pl.ds(e * half_rows, half_rows)
            left, grads = rows[span, 0:width], rows[span, width : 2 * width]
            part[side, t, out, 0 : 2 * strip] = dot(left, wgu[e, :, t * ff : (t + 1) * ff])
            part[side, t, out, 2 * strip : wide] = dot(
                grads, wdn[e, t * strip : (t + 1) * strip, :], 1, 1
            )

    def own_rows(owner):
        return pl.ds(pl.multiple_of(owner * block, block), block)

    def cut(t, way):
        return (0, cuts[t]) if way == 0 else (cuts[t], block - cuts[t])

    def some(start, t, way):
        first, count = cut(t, way)
        return pl.ds(pl.multiple_of(start + first, 16), count)

    def rs_copy(chunk, t, way, step):
        side = lax.rem(chunk, 2)
        src, dst = rs_send.at[side, t, way, step], rs_recv.at[chunk, t, way, step]
        if step == 0:
            src, dst = src.at[pl.ds(*cut(t, way))], dst.at[pl.ds(*cut(t, way))]
        return pltpu.make_async_remote_copy(
            src_ref=src, dst_ref=dst,
            send_sem=rss_sem.at[chunk, t, way, step], recv_sem=rsr_sem.at[chunk, t, way, step],
            device_id=(ctx, (up, down)[way]), device_id_type=MESH,
        )

    def rs_drain(chunk, t):
        for way in range(2):
            for step in range(4):
                rs_copy(chunk, t, way, step).wait_send()

    def rs_step(chunk, t, step):
        side = lax.rem(chunk, 2)
        if step == 0:
            pl.when(chunk >= 2)(lambda: rs_drain(chunk - 2, t))
        for way in range(2):
            owner = lax.rem(tp + (4 - step if way == 0 else 4 + step), RING)
            if step > 0:
                rs_copy(chunk, t, way, step - 1).wait_recv()
            for w in range(2):
                if step == 0 and w != way:
                    continue
                value = part[side, t, some(owner * block, t, w), :]
                here = pl.ds(*cut(t, w))
                if step > 1 or (step == 1 and w == way):
                    value = value + rs_recv[chunk, t, way, step - 1, here, :].astype(F32)
                rs_send[side, t, way, step, here, :] = value.astype(BF)
            rs_copy(chunk, t, way, step).start()

    def act_start(chunk, owner):
        return (owner // 4) * exp_rows + chunk * half_rows + lax.rem(owner, 4) * block

    def act_rows(chunk, owner):
        return pl.ds(pl.multiple_of(act_start(chunk, owner), 16), block)

    def rs_last(chunk, t):
        side = lax.rem(chunk, 2)
        for way in range(2):
            rs_copy(chunk, t, way, 3).wait_recv()

        def total(s):
            cols = slice(s * strip, (s + 1) * strip)
            value = part[side, t, own_rows(tp), cols]
            for way in range(2):
                value = value + rs_recv[chunk, t, way, 3, :, cols].astype(F32)
            return value

        out = act_rows(chunk, tp)
        gate, upper, grad = total(0), total(1), total(2)
        sigma = jax.nn.sigmoid(gate)
        silu = gate * sigma
        act[t, out, 0:strip] = (silu * upper).astype(BF)
        act[t, out, strip : 2 * strip] = (
            grad * upper * sigma * (1.0 + gate * (1.0 - sigma))
        ).astype(BF)
        act[t, out, 2 * strip : wide] = (grad * silu).astype(BF)

    def ag_move(chunk, t, way, step, owner):
        start = act_start(chunk, lax.rem(owner, RING))
        ref = act.at[t, pl.ds(pl.multiple_of(start, 16), block) if step < 3 else some(start, t, way)]
        return pltpu.make_async_remote_copy(
            src_ref=ref, dst_ref=ref,
            send_sem=ags_sem.at[chunk, t, way, step], recv_sem=agr_sem.at[chunk, t, way, step],
            device_id=(ctx, (up, down)[way]), device_id_type=MESH,
        )

    def ag_copy(chunk, t, way, step):
        return ag_move(chunk, t, way, step, tp + (RING - step if way == 0 else step))

    def ag_arrival(chunk, t, way, step):
        return ag_move(chunk, t, way, step, tp + (RING - step - 1 if way == 0 else step + 1))

    def ag_step(chunk, t, step):
        if step == 0:
            rs_last(chunk, t)
        for way in range(2):
            if step > 0:
                ag_arrival(chunk, t, way, step - 1).wait_recv()
            ag_copy(chunk, t, way, step).start()

    def ag_last(chunk, t):
        for way in range(2):
            ag_arrival(chunk, t, way, 3).wait_recv()

    def rows_out(e, span):
        outs = dot(act[0, span, 0:strip], wdn[e, 0:strip, :]) + dot(
            act[1, span, 0:strip], wdn[e, strip : 2 * strip, :]
        )
        grads = dot(act[0, span, strip:wide], wgu[e, :, 0:ff], 1, 1) + dot(
            act[1, span, strip:wide], wgu[e, :, ff : 2 * ff], 1, 1
        )
        return outs, grads

    def pair_rows(q, e):
        start = e * exp_rows + (CHUNKS - 1) * half_rows + q * block
        out = pl.ds(pl.multiple_of(e * block, 16), block)
        outs, grads = rows_out(e, pl.ds(pl.multiple_of(start, 16), block))
        fin[out, 0:width] = outs
        fin[out, width : 2 * width] = grads

    def send_pair(q):
        chunk = CHUNKS - 1
        for b in range(2):
            at = b * cap
            both = jnp.concatenate([fin[at : at + cap, :], fin[block + at : block + at + cap, :]], axis=0)
            x_send[chunk, 2 * q + b] = both.astype(BF)
            back(chunk, b, q).start()

    def finish(chunk):
        ag_last(chunk, 0)
        ag_last(chunk, 1)
        for i in range(SPOTS):
            others(chunk, i, LISTED, lambda i=i: dispatch(chunk, i).wait_send())
        for e in range(2):
            span = pl.ds(pl.multiple_of(e * exp_rows + chunk * half_rows, 16), half_rows)
            out = pl.ds(e * half_rows, half_rows)
            outs, grads = rows_out(e, span)
            fin[out, 0:width] = outs
            fin[out, width : 2 * width] = grads
        for i in range(SPOTS):
            both = jnp.concatenate(
                [
                    fin[i * cap : (i + 1) * cap, :],
                    fin[half_rows + i * cap : half_rows + (i + 1) * cap, :],
                ],
                axis=0,
            )
            x_send[chunk, i] = both.astype(BF)
            others(chunk, i, HELD, lambda i=i: back(chunk, i % 2, i // 2).start())

    build(0)
    pl.semaphore_wait(barrier, n_ctx + 1)
    send_rows(0)
    x_recv[0, self_spot] = x_send[0, core]
    build(1)
    for load in loads[2:]:
        load.wait()
    take_rows(0)
    send_rows(1)
    products(0, 0)

    def turn(c, carry):
        for step in range(4):

            @pl.when(c >= 1)
            def _():
                ag_step(c - 1, 0, step)
                ag_step(c - 1, 1, step)

            rs_step(c, 0, step)
            if step == 0:
                products(c, 1)
            rs_step(c, 1, step)
            if step == 0:
                pl.when(c >= 2)(lambda: finish(c - 2))
            if step == 1:

                @pl.when(c + 2 < CHUNKS)
                def _():
                    build(c + 2)
                    send_rows(c + 2)

            if step == 3:

                @pl.when(c + 1 < CHUNKS)
                def _():
                    take_rows(c + 1)
                    products(c + 1, 0)

        return carry

    lax.fori_loop(0, CHUNKS, turn, 0)

    stores = []

    def store(src, dst):
        stores.append(pltpu.make_async_copy(src, dst, out_sem.at[len(stores)]))
        stores[-1].start()

    def grad_terms(t, e, first, count):
        span = slice(e * exp_rows + first, e * exp_rows + first + count)
        gu = dot(rows[span, 0:width], act[t, span, strip:wide], 0, 0)
        dn = dot(act[t, span, 0:strip], rows[span, width : 2 * width], 0, 0)
        return gu, dn

    ready = (CHUNKS - 1) * half_rows

    def most_grads(t, e):
        gu, dn = grad_terms(t, e, 0, ready)
        gu_sum[t, e], dn_sum[t, e] = gu, dn

    def weight_grads(t, e):
        gu, dn = grad_terms(t, e, ready, exp_rows - ready)
        wgu_st[e, :, t * ff : (t + 1) * ff] = (gu_sum[t, e] + gu).astype(BF)
        for u in range(2):
            store(
                wgu_st.at[e, :, pl.ds(t * ff + u * strip, strip)],
                wgu_out.at[e, :, pl.ds(u * ff + t * strip, strip)],
            )
        at = pl.ds(t * strip, strip)
        wdn_st[e, at, :] = (dn_sum[t, e] + dn).astype(BF)
        store(wdn_st.at[e, at], wdn_out.at[e, at])

    def combine(chunk):
        for i in range(SPOTS):
            others(chunk, i, LISTED, lambda: back_arrival(chunk, i).wait_recv())
        came = r_recv[chunk, :, :, 0:width].reshape(SPOTS * block, width)
        outs = dot(gate_hi[chunk], came, 0, 0) + dot(gate_lo[chunk], came, 0, 0)
        came = r_recv[chunk, :, :, width : 2 * width].reshape(SPOTS * block, width)
        grads = dot(pick_c[chunk], came, 0, 0)
        if chunk > 0:
            outs, grads = acc[:, 0:width] + outs, acc[:, width : 2 * width] + grads
        if chunk < CHUNKS - 1:
            acc[:, 0:width] = outs
            acc[:, width : 2 * width] = grads
        return outs, grads

    last = CHUNKS - 1
    for i in range(SPOTS):
        dispatch(last, i).wait_send()
    def finish_pair(q):
        pair_rows(q, 0)
        pair_rows(q, 1)
        send_pair(q)

    for step in range(4):
        ag_step(last, 0, step)
        ag_step(last, 1, step)
        if step == 0:
            finish(last - 1)
            r_recv[0, core] = x_send[0, self_spot]
        if step == 1:
            combine(0)
            combine(1)
            most_grads(0, 0)
            most_grads(0, 1)
        if step == 2:
            finish_pair(lax.rem(tp + 2, 4))
            most_grads(1, 0)
            most_grads(1, 1)
    finish_pair(lax.rem(tp + 1, 4))
    finish_pair(lax.rem(tp + 3, 4))
    pair_rows(lax.rem(tp, 4), tp // 4)
    ag_last(last, 0)
    ag_last(last, 1)
    pair_rows(lax.rem(tp, 4), 1 - tp // 4)
    send_pair(lax.rem(tp, 4))
    for t in range(2):
        for e in range(2):
            weight_grads(t, e)

    combine(2)
    outs, grads = combine(3)
    moe_out[...] = outs.astype(BF)
    tokens_grad[...] = grads.astype(BF)

    for chunk in range(CHUNKS):
        for t in range(2):
            for way in range(2):
                for step in range(4):
                    ag_copy(chunk, t, way, step).wait_send()
        for i in range(SPOTS):
            others(chunk, i, HELD, lambda i=i, chunk=chunk: back(chunk, i % 2, i // 2).wait_send())
    for chunk in range(CHUNKS - 2, CHUNKS):
        for t in range(2):
            rs_drain(chunk, t)
    for copy in stores:
        copy.wait()


def hand_on(*refs):
    count = (len(refs) - 2) // 3
    came, left = refs[-2:]
    loads, stores = [], []
    for src, dst, mid in zip(refs[:count], refs[count : 2 * count], refs[2 * count : 3 * count]):
        pieces = src.shape[0] if len(src.shape) == 3 else 1
        for piece in range(pieces):
            views = [src, mid, dst]
            if pieces > 1:
                views = [view.at[piece] for view in views]
            loads.append(pltpu.make_async_copy(views[0], views[1], came.at[len(loads)]))
            stores.append(pltpu.make_async_copy(views[1], views[2], left.at[len(stores)]))
            loads[-1].start()
    for load, copy in zip(loads, stores):
        load.wait()
        copy.start()
    for copy in stores:
        copy.wait()


def body(tokens, out_grad, routes, gates, w_gu, w_dn):
    tok, width = tokens.shape
    top = routes.shape[1]
    routes, gates = routes.T, gates.T
    ff = w_dn.shape[1]
    n_ctx = SIDE * SIDE * CORES
    cap = 3 * tok * top // (4 * n_ctx)
    block = 2 * cap
    chunk_rows = SPOTS * block
    all_rows = CHUNKS * chunk_rows
    wide = 3 * ff // 2
    dma = pltpu.SemaphoreType.DMA
    any_space = pl.BlockSpec(memory_space=pl.ANY)
    vmem = pl.BlockSpec(memory_space=pltpu.VMEM)
    flops = 6 * all_rows * width * 3 * ff
    results = pl.pallas_call(
        kernel,
        out_shape=(
            jax.ShapeDtypeStruct((tok, width), BF),
            jax.ShapeDtypeStruct((tok, width), BF),
            jax.ShapeDtypeStruct(w_gu.shape, BF),
            jax.ShapeDtypeStruct(w_dn.shape, BF),
        ),
        in_specs=[any_space] * 6,
        out_specs=(vmem, vmem, any_space, any_space),
        scratch_shapes=[
            pltpu.VMEM(routes.shape, routes.dtype),
            pltpu.VMEM(gates.shape, gates.dtype),
            pltpu.VMEM((tok, 2 * width), BF),
            pltpu.VMEM((all_rows, tok), BF),
            pltpu.VMEM((all_rows, tok), F32),
            pltpu.VMEM((CHUNKS, chunk_rows, tok), BF),
            pltpu.VMEM((CHUNKS, chunk_rows, tok), BF),
            pltpu.VMEM((CHUNKS, chunk_rows, tok), BF),
            pltpu.VMEM((CHUNKS, SPOTS, block, 2 * width), BF),
            pltpu.VMEM((CHUNKS, SPOTS, block, 2 * width), BF),
            pltpu.VMEM((all_rows, 2 * width), BF),
            pltpu.VMEM(w_gu.shape, BF),
            pltpu.VMEM(w_dn.shape, BF),
            pltpu.VMEM((2, 2, chunk_rows, wide), F32),
            pltpu.VMEM((2, 2, 2, 4, block, wide), BF),
            pltpu.VMEM((CHUNKS, 2, 2, 4, block, wide), BF),
            pltpu.VMEM((2, all_rows, wide), BF),
            pltpu.VMEM((chunk_rows, 2 * width), F32),
            pltpu.VMEM((tok, 2 * width), F32),
            pltpu.VMEM((CHUNKS, SPOTS, block, 2 * width), BF),
            pltpu.VMEM(w_gu.shape, BF),
            pltpu.VMEM(w_dn.shape, BF),
            pltpu.VMEM((2, 2, width, ff), F32),
            pltpu.VMEM((2, 2, ff // 2, width), F32),
            dma((9,)),
            dma((CHUNKS, SPOTS)),
            dma((CHUNKS, SPOTS)),
            dma((CHUNKS, 2, 2, 4)),
            dma((CHUNKS, 2, 2, 4)),
            dma((CHUNKS, 2, 2, 4)),
            dma((CHUNKS, 2, 2, 4)),
            dma((CHUNKS, SPOTS)),
            dma((CHUNKS, SPOTS)),
            dma((12,)),
        ],
        compiler_params=pltpu.CompilerParams(
            collective_id=0, has_side_effects=True, vmem_limit_bytes=60 * 1024 * 1024
        ),
        cost_estimate=pl.CostEstimate(flops=flops, bytes_accessed=10 << 20, transcendentals=0),
        name="moe",
    )(tokens, out_grad, routes, gates, w_gu, w_dn)
    return pl.pallas_call(
        hand_on,
        out_shape=tuple(jax.ShapeDtypeStruct(r.shape, r.dtype) for r in results),
        in_specs=[any_space] * 4,
        out_specs=(any_space,) * 4,
        scratch_shapes=[pltpu.VMEM(r.shape, r.dtype) for r in results] + [dma((6,)), dma((6,))],
        compiler_params=pltpu.CompilerParams(vmem_limit_bytes=60 * 1024 * 1024),
        name="hand_on",
    )(*results)


def solution(mesh):
    return jax.shard_map(
        body,
        mesh=mesh,
        in_specs=(
            P("ctx", "tp"),
            P("ctx", "tp"),
            P("ctx", None),
            P("ctx", None),
            P("ctx", "tp", None),
            P("ctx", None, "tp"),
        ),
        out_specs=(P("ctx", "tp"), P("ctx", "tp"), P("ctx", "tp", None), P("ctx", None, "tp")),
        check_vma=False,
    )
```
